32 devices in a mesh: grp: 2 (over x), slab: 16 (over z, y, core).
Axes of the slice: x: 2, y: 2, z: 4, core: 2. Of those that a mesh axis runs over, the one named last changes fastest.
Arguments:
- queries: bfloat16 [4096, 1024], P(('grp', 'slab')), parts along dimension 0, may hold values from 0.0099487305 to 10
- library: bfloat16 [16384, 1024], P(('grp', 'slab')), parts along dimension 0, may hold values from 0.0099487305 to 10
- bucket: int32 [4096, 1], P(('grp', 'slab')), parts along dimension 0, may hold values from 0 to 15; in each aligned block of 128 rows (0 to 127, 128 to 255, ...) at most 16 rows name the same one
- query_charge: int32 [4096], P(('grp', 'slab')), parts along dimension 0, may hold values from 1 to 8
- library_charge: int32 [16384], P(('grp', 'slab')), parts along dimension 0, may hold values from 1 to 8
Outputs:
- scores: bfloat16 [4096, 1536], P(('grp', 'slab')), parts along dimension 0
The draws below stay inside these ranges and needn't reach their ends.
There are 2 independent parts, one for each index of `grp`. The reference program is written for one: setup_inputs(seed, part) draws one part's arguments, and reference() takes and returns one part's arrays. A program takes and returns all parts, laid end to end along the dimension named above; each array names one. Nothing has to cross between parts.
Inputs may be any that keep to these rules, and one draw needn't show every extreme that they name: `bucket`: within the rows of one device (aligned blocks of 128 rows) no slab is named more than 16 times, a bound that some block reaches.
All inputs are finite; a program needn't handle non-finite values.
Results may differ from the reference program's by a relative error of at most 0.0033.
Values may be sent and summed in bfloat16 or wider, within the bound.
No kernel may reach another device: no remote copies, remote signals or barrier semaphores. Data moves between devices by JAX's collectives and lax.ppermute only.
A program may use at most 64 MiB of HBM per device.

```python
import math
import jax
import jax.numpy as jnp
import numpy as np
from jax import lax

D = 1024
CHARGES = 8
Q_DEV = 128
L_DEV = 512
CAP = 16
QUERIES = 2048
LIBRARY = 8192
N_SLAB = 16


def set_ends(drawn, rng, low, top_value):
    dims = drawn.shape
    spot = [jax.random.randint(jax.random.fold_in(rng, axis), (), 0, dims[axis]) for axis in range(len(dims))]
    drawn = drawn.at[tuple(spot)].set(low)
    longest = dims.index(max(dims))
    spot[longest] = (spot[longest] + 1) % dims[longest]
    return drawn.at[tuple(spot)].set(top_value)


def level_of(key, dims, split, smallest, top_value):
    gain, own = 1.0, jax.random.fold_in(key, 6)
    for axis_at, blocks in split:
        steps = jnp.exp(jax.random.uniform(jax.random.fold_in(own, axis_at), (blocks,), jnp.float32, smallest / len(split), top_value / len(split)))
        gain = gain * jnp.repeat(steps, dims[axis_at] // blocks).reshape([-1 if axis == axis_at else 1 for axis in range(len(dims))])
    return gain


def routed_block(own_key, own, number, rows, number_of, top, limit, slope):
    order = jax.random.permutation(own_key, number_of)
    crowded, usual = load_shares(number_of, rows * top, limit, slope, True), load_shares(number_of, rows * top, limit, slope, False)
    places = jnp.arange(number_of)

    def named(sizes, rotation):
        used = int((sizes > 0).sum())
        fixed = max(1, used // 4)
        moved = fixed + (places - fixed + rotation * (used - fixed)) % max(1, number_of - fixed)
        return jnp.zeros((number_of,), jnp.int32).at[order[jnp.where(places < fixed, places, moved)]].set(jnp.asarray(sizes, jnp.int32))

    sizes = jnp.where(number % 4 == 0, named(crowded, number // 4), named(usual, number - number // 4 - 1))
    mixed = jax.random.permutation(jax.random.fold_in(own, 3), number_of)
    donor, taker = mixed[0:number_of // 2 * 2:2], mixed[1:number_of // 2 * 2:2]
    slack = jnp.minimum(sizes[donor] - 1, limit - sizes[taker]) // 2
    slack = jnp.where((donor == order[0]) | (taker == order[0]) | (sizes[taker] == 0), 0, jnp.maximum(slack, 0))
    moved = jax.random.randint(jax.random.fold_in(own, 4), (number_of // 2,), 0, 1 << 20) % (slack + 1)
    sizes = sizes.at[donor].add(-moved).at[taker].add(moved)
    items = jnp.searchsorted(jnp.cumsum(sizes), jnp.arange(rows * top), side="right").astype(jnp.int32)
    table = items.reshape(top, rows).T
    table = table[jax.random.permutation(jax.random.fold_in(own, 1), rows)]
    rotation = jax.random.randint(jax.random.fold_in(own, 2), (rows, 1), 0, top)
    return jnp.take_along_axis(table, (jnp.arange(top)[None, :] + rotation) % top, axis=1)


def load_shares(count, total, reach, lean, full):
    portions = [(1 << 20) // math.isqrt(standing ** lean) + 1 for standing in range(1, count + 1)]
    largest = reach if full else min(reach, max(-(-total // count), total * portions[0] // sum(portions)))
    least = 1 if total - largest >= count - 1 else 0
    holding, spare = [largest] + [least] * (count - 1), total - largest - least * (count - 1)
    while spare > 0:
        free = [i for i in range(1, count) if holding[i] < largest] or [i for i in range(1, count) if holding[i] < reach]
        whole, budget = sum([portions[i] for i in free]), spare
        for i in free:
            addition = min(reach - holding[i], max(1, budget * portions[i] // whole), spare)
            holding[i] = holding[i] + addition
            spare = spare - addition
    return np.array(holding)


def setup_inputs(seed: int = 0, part: int = 0) -> dict:
    arg_keys = jax.random.split(jax.random.key(seed), 6)
    part_keys = jax.random.split(jax.random.fold_in(arg_keys[5], part), 6)
    queries = jnp.clip(jnp.exp(math.log(10.0) - 6.912895 * jax.random.uniform(part_keys[0], (QUERIES, D), jnp.float32) ** level_of(part_keys[0], (QUERIES, D), ((0, 16),), -0.2, 0.2)), 0.0099487305, 10.0).astype(jnp.bfloat16)
    library = jnp.clip(jnp.exp(math.log(10.0) - 6.912895 * jax.random.uniform(part_keys[1], (LIBRARY, D), jnp.float32) ** level_of(part_keys[1], (LIBRARY, D), ((0, 16),), -0.2, 0.2)), 0.0099487305, 10.0).astype(jnp.bfloat16)
    bucket_keys = jax.random.split(jax.random.fold_in(part_keys[2], 1), QUERIES // Q_DEV)
    bucket_turns = jax.random.permutation(jax.random.fold_in(part_keys[2], 3), QUERIES // Q_DEV)
    bucket = jax.vmap(lambda own, number: routed_block(jax.random.fold_in(part_keys[2], 2), own, number, Q_DEV, N_SLAB, 1, CAP, 2))(bucket_keys, bucket_turns).reshape((QUERIES, 1))
    query_charge = set_ends(jax.random.randint(part_keys[3], (QUERIES,), 1, CHARGES + 1), jax.random.fold_in(part_keys[3], 1), 1, CHARGES).astype(jnp.int32)
    library_charge = set_ends(jax.random.randint(part_keys[4], (LIBRARY,), 1, CHARGES + 1), jax.random.fold_in(part_keys[4], 1), 1, CHARGES).astype(jnp.int32)
    return {"queries": queries, "library": library, "bucket": bucket, "query_charge": query_charge, "library_charge": library_charge}


EPS = 1e-06

def normalize(rows):
    values = rows.astype(jnp.float32)
    return (values * lax.rsqrt(lax.optimization_barrier(jnp.sum(values * values, axis=-1, keepdims=True)) + EPS)).astype(jnp.bfloat16)

def reference(queries, library, bucket, query_charge, library_charge):
    query_unit = normalize(queries)
    library_unit = normalize(library).reshape(N_SLAB, L_DEV, D)
    lib_charges = library_charge.reshape(N_SLAB, L_DEV)
    target = bucket[:, 0]
    slots = 2 * Q_DEV

    def step(result, slab_id):
        found = jnp.nonzero(target == slab_id, size=slots, fill_value=QUERIES)[0].astype(jnp.int32)
        safe = jnp.minimum(found, QUERIES - 1)
        rows = query_unit[safe]
        row_charge = query_charge[safe].astype(jnp.float32)
        window_ids = jnp.stack([(slab_id - 1) % N_SLAB, slab_id, (slab_id + 1) % N_SLAB]).astype(jnp.int32)
        window = library_unit[window_ids].reshape(3 * L_DEV, D)
        window_charge = lib_charges[window_ids].reshape(3 * L_DEV).astype(jnp.float32)
        raw = jnp.dot(rows, window.T, preferred_element_type=jnp.float32)
        keep = jnp.abs(row_charge[:, None] - window_charge[None, :]) <= 2.0
        valued = jnp.where(keep, raw, 0.0).astype(jnp.bfloat16)
        return (result.at[found].set(valued, mode='drop'), None)
    start = jnp.zeros((QUERIES, 3 * L_DEV), jnp.bfloat16)
    result, unused = lax.scan(step, start, jnp.arange(N_SLAB, dtype=jnp.int32))
    return result
```

```python
import functools

import jax
import jax.numpy as jnp
from jax import lax
from jax.experimental import pallas as pl
from jax.experimental.pallas import tpu as pltpu
from jax.sharding import PartitionSpec as P

EPS = 1e-06
PLANE = 4
CAP = 16
META = 16
F32 = jnp.float32
BF16 = jnp.bfloat16


def passed_along(value, axis, steps):
    count = lax.axis_size(axis)
    pairs = [(source, (source + steps) % count) for source in range(count)]
    return lax.ppermute(value, axis, pairs)


def normalize(rows):
    values = rows.astype(F32)
    return (values * lax.rsqrt(jnp.sum(values * values, axis=-1, keepdims=True) + EPS)).astype(BF16)


def score_block(rows, row_charge, lib_rows, lib_charge):
    raw = lax.dot_general(rows, lib_rows, (((1,), (1,)), ((), ())), preferred_element_type=F32)
    keep = jnp.abs(row_charge.astype(F32)[:, None] - lib_charge.astype(F32)[None, :]) <= 2.0
    return jnp.where(keep, raw, 0.0).astype(BF16)


def selector(slot_ids, total):
    places = jnp.arange(total, dtype=jnp.int32)
    return (places[:, None] == slot_ids[None, :]).astype(BF16)


def pick_rows(select, flat):
    return lax.dot_general(
        select, flat, (((0,), (0,)), ((), ())), preferred_element_type=F32
    ).astype(BF16)


def place_rows(select, values):
    return jnp.dot(select, values, preferred_element_type=F32).astype(BF16)


def general_plan(queries, library, bucket, query_charge, library_charge):
    n_slab = lax.axis_size("slab")
    q_rows = queries.shape[0]
    width = queries.shape[1]
    cap = 2 * q_rows // n_slab
    query_unit = normalize(queries)
    library_unit = normalize(library)
    lib_charge = library_charge.astype(BF16)
    qcharge_col = query_charge.astype(BF16)[:, None]
    target = bucket[:, 0]
    positions = jnp.arange(q_rows, dtype=jnp.int32)
    earlier = (target[:, None] == target[None, :]) & (positions[None, :] < positions[:, None])
    rank = jnp.sum(earlier.astype(jnp.int32), axis=1)
    select_home = selector(target * cap + rank, n_slab * cap)
    outgoing = place_rows(select_home, query_unit).reshape(n_slab, cap, width)
    out_charge = place_rows(select_home, qcharge_col).reshape(n_slab, cap)
    below_rows, below_charge = passed_along((library_unit, lib_charge), "slab", 1)
    above_rows, above_charge = passed_along((library_unit, lib_charge), "slab", -1)
    rows = lax.all_to_all(outgoing, "slab", split_axis=0, concat_axis=0, tiled=True)
    charges = lax.all_to_all(out_charge, "slab", split_axis=0, concat_axis=0, tiled=True)
    count = rows.shape[1]
    flat = rows.reshape(n_slab * count, width)
    flat_charge = charges.reshape(n_slab * count)
    middle = score_block(flat, flat_charge, library_unit, lib_charge)
    lower = score_block(flat, flat_charge, below_rows, below_charge)
    upper = score_block(flat, flat_charge, above_rows, above_charge)
    joined = jnp.concatenate([lower, middle, upper], axis=1)
    joined = joined.reshape(n_slab, count, joined.shape[1])
    returned = lax.all_to_all(joined, "slab", split_axis=0, concat_axis=0, tiled=True)
    flat_back = returned.reshape(returned.shape[0] * returned.shape[1], returned.shape[2])
    return pick_rows(select_home, flat_back)


def swapped(value, mask):
    count = lax.axis_size("slab")
    return lax.ppermute(value, "slab", [(i, i ^ mask) for i in range(count)])


def unit_rows(values):
    values = values.astype(F32)
    return (values * lax.rsqrt(jnp.sum(values * values, axis=-1, keepdims=True) + EPS)).astype(BF16)


def query_kernel(q_ref, bucket_ref, charge_ref, a_ref, b_ref, slot_ref):
    q_rows, width = q_ref.shape
    half = width // 2
    unit = unit_rows(q_ref[...])
    for k in range(0, half, 128):
        a_ref[k // 128 * q_rows : (k // 128 + 1) * q_rows, :] = unit[:, k : k + 128]
        b_ref[k // 128 * q_rows : (k // 128 + 1) * q_rows, :] = unit[:, half + k : half + k + 128]
    along = jnp.broadcast_to(bucket_ref[...].astype(F32), (q_rows, q_rows))
    down = along.T
    i = lax.broadcasted_iota(jnp.int32, (q_rows, q_rows), 0)
    j = lax.broadcasted_iota(jnp.int32, (q_rows, q_rows), 1)
    earlier = jnp.where((along == down) & (i < j), 1.0, 0.0)
    rank = jnp.sum(earlier, axis=0, keepdims=True)
    slot = bucket_ref[...].astype(F32) * CAP + rank
    slot_ref[...] = slot.astype(jnp.int32)
    line = lax.broadcasted_iota(jnp.int32, (META, q_rows), 0)
    charge = charge_ref[...].astype(F32)
    meta = jnp.where(line == 0, slot, jnp.where(line == 1, charge, 0.0))
    a_ref[half // 128 * q_rows :, :] = meta.astype(BF16)


def library_kernel(lib_ref, charge_ref, a_ref, b_ref):
    rows, width = lib_ref.shape
    half = rows // 2
    for start in range(0, half, 64):
        a_ref[start : start + 64, :] = unit_rows(lib_ref[start : start + 64, :])
        b_ref[start : start + 64, :] = unit_rows(lib_ref[half + start : half + start + 64, :])
    charge = jnp.broadcast_to(charge_ref[...].astype(F32), (META, rows)).astype(BF16)
    a_ref[half:, :] = jnp.zeros((META, width), BF16)
    a_ref[half:, :rows] = charge


def place_kernel(me_ref, *refs):
    x_ref, charge_ref = refs[8:]
    n_slots = (PLANE + 2) * CAP
    q_rows = refs[1].shape[1]
    total = 4 * PLANE * CAP
    first = (me_ref[0] // PLANE * PLANE - 1) * CAP
    for k in range(4):
        a_ref, b_ref = refs[2 * k], refs[2 * k + 1]
        n_chunk = b_ref.shape[0] // q_rows
        meta = a_ref[n_chunk * q_rows :, :].astype(F32)
        rel = meta[0:1, :].astype(jnp.int32) - first + total
        rel = jnp.where(rel >= total, rel - total, rel)
        rel = jnp.where(rel >= total, rel - total, rel)
        place = lax.broadcasted_iota(jnp.int32, (n_slots, q_rows), 0) == rel
        charge = jnp.sum(jnp.where(place, meta[1:2, :], 0.0), axis=1, keepdims=True)
        charge_ref[k * n_slots : (k + 1) * n_slots, :] = jnp.broadcast_to(charge, (n_slots, 128))
        select = jnp.where(place, 1.0, 0.0).astype(BF16)
        for n in range(2 * n_chunk):
            ref = a_ref if n < n_chunk else b_ref
            at = n % n_chunk * q_rows
            x_ref[k * n_slots : (k + 1) * n_slots, n * 128 : (n + 1) * 128] = jnp.dot(
                select, ref[at : at + q_rows, :], preferred_element_type=F32
            ).astype(BF16)


def score_slabs(slabs, x_ref, charge_ref, lib_refs, out_refs, rows_ref, rcharge_ref):
    n_slots = (PLANE + 2) * CAP
    seen = 3 * CAP
    for n, slab in enumerate(slabs):
        a_ref, b_ref = lib_refs[2 * n], lib_refs[2 * n + 1]
        half = b_ref.shape[0]
        for k in range(4):
            at = pl.multiple_of(slab * CAP + k * n_slots, CAP)
            rows_ref[k * seen : (k + 1) * seen, :] = x_ref[pl.ds(at, seen), :]
            rcharge_ref[k * seen : (k + 1) * seen, :] = charge_ref[pl.ds(at, seen), :]
        row_charge = rcharge_ref[:, 0:1]
        for part, ref in enumerate((a_ref, b_ref)):
            lib_charge = a_ref[half:, part * half : (part + 1) * half].astype(F32)[0:1, :]
            raw = lax.dot_general(
                rows_ref[...], ref[:half, :], (((1,), (1,)), ((), ())), preferred_element_type=F32
            )
            kept = jnp.where(jnp.abs(row_charge - lib_charge) <= 2.0, raw, 0.0).astype(BF16)
            for k in range(4):
                out_refs[k][n * seen : (n + 1) * seen, part * half : (part + 1) * half] = kept[
                    k * seen : (k + 1) * seen, :
                ]


def near_kernel(me_ref, *refs):
    q_refs, lib_refs = refs[:8], refs[8:12]
    out_refs, x_ref, charge_ref = refs[12:16], refs[16], refs[17]
    place_kernel(me_ref, *q_refs, x_ref, charge_ref)
    own = me_ref[0] % PLANE
    score_slabs((own, own ^ 1), x_ref, charge_ref, lib_refs, out_refs, *refs[18:])


def far_kernel(me_ref, *refs):
    x_ref, charge_ref, lib_refs, out_refs = refs[0], refs[1], refs[2:6], refs[6:10]
    own = me_ref[0] % PLANE
    score_slabs((own ^ 2, own ^ 3), x_ref, charge_ref, lib_refs, out_refs, *refs[10:])


def home_kernel(me_ref, slot_ref, *refs):
    near, far, out_ref, flat_ref = refs[:4], refs[4:8], refs[8], refs[9]
    q_rows = slot_ref.shape[1]
    l_rows = near[0].shape[1]
    n_slab = 4 * PLANE
    total = n_slab * CAP
    slot = slot_ref[...]
    bucket, rank = slot // CAP, slot % CAP
    places = lax.broadcasted_iota(jnp.int32, (total, q_rows), 0)
    for unit in range(3):
        for m in range(n_slab):
            ref = (far if m & 2 else near)[m // PLANE]
            at = (m & 1) * 3 * CAP + (2 - unit) * CAP
            flat_ref[m * CAP : (m + 1) * CAP, :] = ref[at : at + CAP, :]
        slab = (bucket + (unit - 1 + n_slab)) % n_slab
        want = (slab ^ me_ref[0]) * CAP + rank
        select = jnp.where(places == want, 1.0, 0.0).T.astype(BF16)
        out_ref[:, unit * l_rows : (unit + 1) * l_rows] = jnp.dot(
            select, flat_ref[...], preferred_element_type=F32
        ).astype(BF16)


VMEM = pl.BlockSpec(memory_space=pltpu.VMEM)
SMEM = pl.BlockSpec(memory_space=pltpu.SMEM)


def kernel_call(body, outs, args, scratch=(), scalars=0, flops=0):
    size = sum(a.size * a.dtype.itemsize for a in [*args, *outs])
    return pl.pallas_call(
        body,
        out_shape=[jax.ShapeDtypeStruct(o.shape, o.dtype) for o in outs],
        in_specs=[SMEM] * scalars + [VMEM] * (len(args) - scalars),
        out_specs=[VMEM] * len(outs),
        scratch_shapes=scratch,
        compiler_params=pltpu.CompilerParams(vmem_limit_bytes=16 * 1024 * 1024),
        cost_estimate=pl.CostEstimate(flops=flops, bytes_accessed=size, transcendentals=0),
    )(*args)


def shape(*dims, dtype=BF16):
    return jax.ShapeDtypeStruct(dims, dtype)


def line_plan(queries, library, bucket, query_charge, library_charge):
    q_rows, width = queries.shape
    l_rows = library.shape[0]
    me = lax.axis_index("slab").astype(jnp.int32).reshape(1)
    half = width // 2 // 128 * q_rows
    qa, qb, slot = kernel_call(
        query_kernel,
        [shape(half + META, 128), shape(half, 128), shape(1, q_rows, dtype=jnp.int32)],
        [queries, bucket.reshape(1, q_rows), query_charge.reshape(1, q_rows)],
    )
    la, lb = kernel_call(
        library_kernel,
        [shape(l_rows // 2 + META, width), shape(l_rows // 2, width)],
        [library, library_charge.reshape(1, l_rows)],
    )
    q12a, q12b = swapped(qa, 12), swapped(qb, 12)
    q4a, q4b = swapped(qa, 4), swapped(qb, 4)
    q8a, q8b = swapped(q12a, 4), swapped(q12b, 4)
    ya, yb = swapped(la, 2), swapped(lb, 2)
    ca, cb = swapped(la, 1), swapped(lb, 1)
    da, db = swapped(ya, 1), swapped(yb, 1)
    n_slots, seen = (PLANE + 2) * CAP, 3 * CAP
    blocks = [shape(2 * seen, l_rows)] * 4
    scratch = [pltpu.VMEM((4 * seen, width), BF16), pltpu.VMEM((4 * seen, 128), F32)]
    *near, x, x_charge = kernel_call(
        near_kernel,
        blocks + [shape(4 * n_slots, width), shape(4 * n_slots, 128, dtype=F32)],
        [me, qa, qb, q4a, q4b, q8a, q8b, q12a, q12b, la, lb, ca, cb],
        scratch,
        scalars=1,
    )
    near_back = [near[0]] + [swapped(near[k], 4 * k) for k in (1, 2, 3)]
    far = kernel_call(far_kernel, blocks, [me, x, x_charge, ya, yb, da, db], scratch, scalars=1)
    far_back = [far[0]] + [swapped(far[k], 4 * k) for k in (1, 2, 3)]
    (out,) = kernel_call(
        home_kernel,
        [shape(q_rows, 3 * l_rows)],
        [me, slot, *near_back, *far_back],
        [pltpu.VMEM((4 * PLANE * CAP, l_rows), BF16)],
        scalars=1,
    )
    return out


def per_device(queries, library, bucket, query_charge, library_charge):
    n_slab = lax.axis_size("slab")
    q_rows, width = queries.shape
    fits = n_slab == 4 * PLANE and 2 * q_rows == n_slab * CAP and q_rows == 128
    plan = line_plan if fits and width % 256 == 0 and library.shape[0] <= width else general_plan
    return plan(queries, library, bucket, query_charge, library_charge)


def solution(mesh):
    placed = (
        P(("grp", "slab"), None),
        P(("grp", "slab"), None),
        P(("grp", "slab"), None),
        P(("grp", "slab")),
        P(("grp", "slab")),
    )
    return jax.shard_map(
        per_device, mesh=mesh, in_specs=placed, out_specs=P(("grp", "slab"), None), check_vma=False
    )
```

```python
import functools

import jax
import jax.numpy as jnp
from jax import lax
from jax.experimental import pallas as pl
from jax.experimental.pallas import tpu as pltpu
from jax.sharding import PartitionSpec as P

EPS = 1e-06
PLANE = 4
CAP = 16
META = 16
F32 = jnp.float32
BF16 = jnp.bfloat16


def passed_along(value, axis, steps):
    count = lax.axis_size(axis)
    pairs = [(source, (source + steps) % count) for source in range(count)]
    return lax.ppermute(value, axis, pairs)


def normalize(rows):
    values = rows.astype(F32)
    return (values * lax.rsqrt(jnp.sum(values * values, axis=-1, keepdims=True) + EPS)).astype(BF16)


def score_block(rows, row_charge, lib_rows, lib_charge):
    raw = lax.dot_general(rows, lib_rows, (((1,), (1,)), ((), ())), preferred_element_type=F32)
    keep = jnp.abs(row_charge.astype(F32)[:, None] - lib_charge.astype(F32)[None, :]) <= 2.0
    return jnp.where(keep, raw, 0.0).astype(BF16)


def selector(slot_ids, total):
    places = jnp.arange(total, dtype=jnp.int32)
    return (places[:, None] == slot_ids[None, :]).astype(BF16)


def pick_rows(select, flat):
    return lax.dot_general(
        select, flat, (((0,), (0,)), ((), ())), preferred_element_type=F32
    ).astype(BF16)


def place_rows(select, values):
    return jnp.dot(select, values, preferred_element_type=F32).astype(BF16)


def general_plan(queries, library, bucket, query_charge, library_charge):
    n_slab = lax.axis_size("slab")
    q_rows = queries.shape[0]
    width = queries.shape[1]
    cap = 2 * q_rows // n_slab
    query_unit = normalize(queries)
    library_unit = normalize(library)
    lib_charge = library_charge.astype(BF16)
    qcharge_col = query_charge.astype(BF16)[:, None]
    target = bucket[:, 0]
    positions = jnp.arange(q_rows, dtype=jnp.int32)
    earlier = (target[:, None] == target[None, :]) & (positions[None, :] < positions[:, None])
    rank = jnp.sum(earlier.astype(jnp.int32), axis=1)
    select_home = selector(target * cap + rank, n_slab * cap)
    outgoing = place_rows(select_home, query_unit).reshape(n_slab, cap, width)
    out_charge = place_rows(select_home, qcharge_col).reshape(n_slab, cap)
    below_rows, below_charge = passed_along((library_unit, lib_charge), "slab", 1)
    above_rows, above_charge = passed_along((library_unit, lib_charge), "slab", -1)
    rows = lax.all_to_all(outgoing, "slab", split_axis=0, concat_axis=0, tiled=True)
    charges = lax.all_to_all(out_charge, "slab", split_axis=0, concat_axis=0, tiled=True)
    count = rows.shape[1]
    flat = rows.reshape(n_slab * count, width)
    flat_charge = charges.reshape(n_slab * count)
    middle = score_block(flat, flat_charge, library_unit, lib_charge)
    lower = score_block(flat, flat_charge, below_rows, below_charge)
    upper = score_block(flat, flat_charge, above_rows, above_charge)
    joined = jnp.concatenate([lower, middle, upper], axis=1)
    joined = joined.reshape(n_slab, count, joined.shape[1])
    returned = lax.all_to_all(joined, "slab", split_axis=0, concat_axis=0, tiled=True)
    flat_back = returned.reshape(returned.shape[0] * returned.shape[1], returned.shape[2])
    return pick_rows(select_home, flat_back)


def swapped(value, mask):
    count = lax.axis_size("slab")
    return lax.ppermute(value, "slab", [(i, i ^ mask) for i in range(count)])


def unit_rows(values):
    values = values.astype(F32)
    return (values * lax.rsqrt(jnp.sum(values * values, axis=-1, keepdims=True) + EPS)).astype(BF16)


def prep_kernel(me_ref, q_hbm, lib_hbm, bucket_hbm, qcharge_hbm, lcharge_hbm, *refs):
    out_refs, lib_out, slot_ref = refs[:4], refs[4], refs[5]
    q_ref, lib_ref, bucket_ref, qcharge_ref, lcharge_ref, sem = refs[6:]
    copies = [
        pltpu.make_async_copy(source, target, sem.at[n])
        for n, (source, target) in enumerate(
            [
                (bucket_hbm, bucket_ref),
                (qcharge_hbm, qcharge_ref),
                (q_hbm, q_ref),
                (lcharge_hbm, lcharge_ref),
                (lib_hbm, lib_ref),
            ]
        )
    ]
    for copy in copies:
        copy.start()
    q_rows, width = q_ref.shape
    n_slots = (PLANE + 2) * CAP
    total = 4 * PLANE * CAP
    copies[0].wait()
    copies[1].wait()
    bucket = bucket_ref[...]
    along = jnp.broadcast_to(bucket.astype(F32), (q_rows, q_rows))
    i = lax.broadcasted_iota(jnp.int32, (q_rows, q_rows), 0)
    j = lax.broadcasted_iota(jnp.int32, (q_rows, q_rows), 1)
    earlier = jnp.where((along == along.T) & (i < j), 1.0, 0.0)
    rank = jnp.sum(earlier, axis=0, keepdims=True)
    slot = bucket * CAP + rank.astype(jnp.int32)
    slot_ref[...] = slot
    charge = jnp.broadcast_to(qcharge_ref[...].astype(F32), (META, q_rows)).astype(BF16)
    copies[2].wait()
    unit = unit_rows(q_ref[...])
    for k in range(4):
        plane = (me_ref[0] // PLANE) ^ k
        rel = (slot + (total - (plane * PLANE - 1) * CAP)) % total
        place = lax.broadcasted_iota(jnp.int32, (q_rows, q_rows), 0) == rel
        select = jnp.where(place, 1.0, 0.0).astype(BF16)
        rows = jnp.dot(select[:n_slots, :], unit, preferred_element_type=F32).astype(BF16)
        for n in range(width // 128):
            out_refs[k][n * n_slots : (n + 1) * n_slots, :] = rows[:, n * 128 : (n + 1) * 128]
        placed = lax.dot_general(
            charge, select, (((1,), (1,)), ((), ())), preferred_element_type=F32
        )
        out_refs[k][width // 128 * n_slots :, :] = placed.astype(BF16)
    copies[3].wait()
    copies[4].wait()
    rows = lib_ref.shape[0]
    for start in range(0, rows, 64):
        lib_out[start : start + 64, :] = unit_rows(lib_ref[start : start + 64, :])
    lib_out[rows:, :] = jnp.zeros((META, width), BF16)
    lib_out[rows:, :rows] = jnp.broadcast_to(lcharge_ref[...].astype(F32), (META, rows)).astype(BF16)


def score_kernel(turn, me_ref, *refs):
    q_refs, lib_refs, out_refs, rows_ref, charge_ref = refs[:4], refs[4:6], refs[6:10], refs[10], refs[11]
    n_slots, seen = (PLANE + 2) * CAP, 3 * CAP
    for n, lib in enumerate(lib_refs):
        width = lib.shape[1]
        l_rows = lib.shape[0] - META
        at = pl.multiple_of(((me_ref[0] % PLANE) ^ (turn ^ n)) * CAP, CAP)
        for k in range(4):
            for c in range(width // 128):
                rows_ref[k * seen : (k + 1) * seen, c * 128 : (c + 1) * 128] = q_refs[k][
                    pl.ds(pl.multiple_of(at + c * n_slots, CAP), seen), :
                ]
            if n == 0:
                line = q_refs[k][width // 128 * n_slots :, :].astype(F32)[0:1, :]
                charge_ref[k] = jnp.broadcast_to(line, (128, 128)).T
        lib_charge = lib[l_rows:, :l_rows].astype(F32)[0:1, :]
        raw = lax.dot_general(
            rows_ref[...], lib[:l_rows, :], (((1,), (1,)), ((), ())), preferred_element_type=F32
        )
        for k in range(4):
            row_charge = charge_ref[k, pl.ds(at, seen), :][:, 0:1]
            kept = jnp.abs(row_charge - lib_charge) <= 2.0
            out_refs[k][n * seen : (n + 1) * seen, :] = jnp.where(
                kept, raw[k * seen : (k + 1) * seen, :], 0.0
            ).astype(BF16)


def home_kernel(me_ref, slot_ref, *refs):
    near, far, out_ref, flat_ref = refs[:4], refs[4:8], refs[8], refs[9]
    q_rows = slot_ref.shape[1]
    l_rows = near[0].shape[1]
    n_slab = 4 * PLANE
    total = n_slab * CAP
    slot = slot_ref[...]
    bucket, rank = slot // CAP, slot % CAP
    places = lax.broadcasted_iota(jnp.int32, (total, q_rows), 0)
    for unit in range(3):
        for m in range(n_slab):
            ref = (far if m & 2 else near)[m // PLANE]
            at = (m & 1) * 3 * CAP + (2 - unit) * CAP
            flat_ref[m * CAP : (m + 1) * CAP, :] = ref[at : at + CAP, :]
        slab = (bucket + (unit - 1 + n_slab)) % n_slab
        want = (slab ^ me_ref[0]) * CAP + rank
        select = jnp.where(places == want, 1.0, 0.0).T.astype(BF16)
        out_ref[:, unit * l_rows : (unit + 1) * l_rows] = jnp.dot(
            select, flat_ref[...], preferred_element_type=F32
        ).astype(BF16)


VMEM = pl.BlockSpec(memory_space=pltpu.VMEM)
SMEM = pl.BlockSpec(memory_space=pltpu.SMEM)
HBM = pl.BlockSpec(memory_space=pltpu.HBM)


def kernel_call(body, outs, args, specs, scratch=(), flops=0):
    size = sum(a.size * a.dtype.itemsize for a in [*args, *outs])
    return pl.pallas_call(
        body,
        out_shape=[jax.ShapeDtypeStruct(o.shape, o.dtype) for o in outs],
        in_specs=specs,
        out_specs=[VMEM] * len(outs),
        scratch_shapes=scratch,
        compiler_params=pltpu.CompilerParams(vmem_limit_bytes=12 * 1024 * 1024),
        cost_estimate=pl.CostEstimate(flops=flops, bytes_accessed=size, transcendentals=0),
    )(*args)


def shape(*dims, dtype=BF16):
    return jax.ShapeDtypeStruct(dims, dtype)


def line_plan(queries, library, bucket, query_charge, library_charge):
    q_rows, width = queries.shape
    l_rows = library.shape[0]
    me = lax.axis_index("slab").astype(jnp.int32).reshape(1)
    n_slots, seen = (PLANE + 2) * CAP, 3 * CAP
    int32 = jnp.int32
    q0, q4, q8, q12, lib, slot = kernel_call(
        prep_kernel,
        [shape(width // 128 * n_slots + META, 128)] * 4
        + [shape(l_rows + META, width), shape(1, q_rows, dtype=int32)],
        [
            me,
            queries,
            library,
            bucket.reshape(1, q_rows),
            query_charge.reshape(1, q_rows),
            library_charge.reshape(1, l_rows),
        ],
        [SMEM] + [HBM] * 5,
        [
            pltpu.VMEM((q_rows, width), BF16),
            pltpu.VMEM((l_rows, width), BF16),
            pltpu.VMEM((1, q_rows), int32),
            pltpu.VMEM((1, q_rows), int32),
            pltpu.VMEM((1, l_rows), int32),
            pltpu.SemaphoreType.DMA((5,)),
        ],
    )
    q12, q8, q4 = swapped(q12, 12), swapped(q8, 8), swapped(q4, 4)
    lib_y, lib_c = swapped(lib, 2), swapped(lib, 1)
    scratch = [pltpu.VMEM((4 * seen, width), BF16), pltpu.VMEM((4, 128, 128), F32)]

    def scores(turn, one, other):
        blocks = kernel_call(
            functools.partial(score_kernel, turn),
            [shape(2 * seen, l_rows)] * 4,
            [me, q0, q4, q8, q12, one, other],
            [SMEM] + [VMEM] * 6,
            scratch,
            flops=2 * 2 * 4 * seen * l_rows * width,
        )
        far, middle, close = swapped(blocks[3], 12), swapped(blocks[2], 8), swapped(blocks[1], 4)
        return [blocks[0], close, middle, far]

    near = scores(0, lib, lib_c)
    lib_y, near[0] = lax.optimization_barrier((lib_y, near[0]))
    lib_d = swapped(lib_y, 1)
    far = scores(2, lib_y, lib_d)
    (out,) = kernel_call(
        home_kernel,
        [shape(q_rows, 3 * l_rows)],
        [me, slot, *near, *far],
        [SMEM] + [VMEM] * 9,
        [pltpu.VMEM((4 * PLANE * CAP, l_rows), BF16)],
    )
    return out


def per_device(queries, library, bucket, query_charge, library_charge):
    n_slab = lax.axis_size("slab")
    q_rows, width = queries.shape
    fits = n_slab == 4 * PLANE and 2 * q_rows == n_slab * CAP and q_rows == 128
    plan = line_plan if fits and width % 256 == 0 and library.shape[0] <= width else general_plan
    return plan(queries, library, bucket, query_charge, library_charge)


def solution(mesh):
    placed = (
        P(("grp", "slab"), None),
        P(("grp", "slab"), None),
        P(("grp", "slab"), None),
        P(("grp", "slab")),
        P(("grp", "slab")),
    )
    return jax.shard_map(
        per_device, mesh=mesh, in_specs=placed, out_specs=P(("grp", "slab"), None), check_vma=False
    )
```

```python
import functools

import jax
import jax.numpy as jnp
from jax import lax
from jax.experimental import pallas as pl
from jax.experimental.pallas import tpu as pltpu
from jax.sharding import PartitionSpec as P

EPS = 1e-06
PLANE = 4
CAP = 16
META = 16
PREP_LIMIT = 12 * 1024 * 1024
COST = 1
F32 = jnp.float32
BF16 = jnp.bfloat16


def passed_along(value, axis, steps):
    count = lax.axis_size(axis)
    pairs = [(source, (source + steps) % count) for source in range(count)]
    return lax.ppermute(value, axis, pairs)


def normalize(rows):
    values = rows.astype(F32)
    return (values * lax.rsqrt(jnp.sum(values * values, axis=-1, keepdims=True) + EPS)).astype(BF16)


def score_block(rows, row_charge, lib_rows, lib_charge):
    raw = lax.dot_general(rows, lib_rows, (((1,), (1,)), ((), ())), preferred_element_type=F32)
    keep = jnp.abs(row_charge.astype(F32)[:, None] - lib_charge.astype(F32)[None, :]) <= 2.0
    return jnp.where(keep, raw, 0.0).astype(BF16)


def selector(slot_ids, total):
    places = jnp.arange(total, dtype=jnp.int32)
    return (places[:, None] == slot_ids[None, :]).astype(BF16)


def pick_rows(select, flat):
    return lax.dot_general(
        select, flat, (((0,), (0,)), ((), ())), preferred_element_type=F32
    ).astype(BF16)


def place_rows(select, values):
    return jnp.dot(select, values, preferred_element_type=F32).astype(BF16)


def general_plan(queries, library, bucket, query_charge, library_charge):
    n_slab = lax.axis_size("slab")
    q_rows = queries.shape[0]
    width = queries.shape[1]
    cap = 2 * q_rows // n_slab
    query_unit = normalize(queries)
    library_unit = normalize(library)
    lib_charge = library_charge.astype(BF16)
    qcharge_col = query_charge.astype(BF16)[:, None]
    target = bucket[:, 0]
    positions = jnp.arange(q_rows, dtype=jnp.int32)
    earlier = (target[:, None] == target[None, :]) & (positions[None, :] < positions[:, None])
    rank = jnp.sum(earlier.astype(jnp.int32), axis=1)
    select_home = selector(target * cap + rank, n_slab * cap)
    outgoing = place_rows(select_home, query_unit).reshape(n_slab, cap, width)
    out_charge = place_rows(select_home, qcharge_col).reshape(n_slab, cap)
    below_rows, below_charge = passed_along((library_unit, lib_charge), "slab", 1)
    above_rows, above_charge = passed_along((library_unit, lib_charge), "slab", -1)
    rows = lax.all_to_all(outgoing, "slab", split_axis=0, concat_axis=0, tiled=True)
    charges = lax.all_to_all(out_charge, "slab", split_axis=0, concat_axis=0, tiled=True)
    count = rows.shape[1]
    flat = rows.reshape(n_slab * count, width)
    flat_charge = charges.reshape(n_slab * count)
    middle = score_block(flat, flat_charge, library_unit, lib_charge)
    lower = score_block(flat, flat_charge, below_rows, below_charge)
    upper = score_block(flat, flat_charge, above_rows, above_charge)
    joined = jnp.concatenate([lower, middle, upper], axis=1)
    joined = joined.reshape(n_slab, count, joined.shape[1])
    returned = lax.all_to_all(joined, "slab", split_axis=0, concat_axis=0, tiled=True)
    flat_back = returned.reshape(returned.shape[0] * returned.shape[1], returned.shape[2])
    return pick_rows(select_home, flat_back)


def swapped(value, mask):
    count = lax.axis_size("slab")
    return lax.ppermute(value, "slab", [(i, i ^ mask) for i in range(count)])


def unit_rows(values):
    values = values.astype(F32)
    return (values * lax.rsqrt(jnp.sum(values * values, axis=-1, keepdims=True) + EPS)).astype(BF16)


def prep_kernel(me_ref, q_hbm, bucket_hbm, qcharge_hbm, lcharge_hbm, *refs):
    out_refs, slot_ref, lcharge_out = refs[:4], refs[4], refs[5]
    q_ref, bucket_ref, qcharge_ref, lcharge_ref, sem = refs[6:]
    copies = [
        pltpu.make_async_copy(source, target, sem.at[n])
        for n, (source, target) in enumerate(
            [
                (bucket_hbm, bucket_ref),
                (qcharge_hbm, qcharge_ref),
                (q_hbm, q_ref),
                (lcharge_hbm, lcharge_ref),
            ]
        )
    ]
    for copy in copies:
        copy.start()
    q_rows, width = q_ref.shape
    n_slots = (PLANE + 2) * CAP
    total = 4 * PLANE * CAP
    copies[0].wait()
    copies[1].wait()
    bucket = bucket_ref[...]
    along = jnp.broadcast_to(bucket.astype(F32), (q_rows, q_rows))
    i = lax.broadcasted_iota(jnp.int32, (q_rows, q_rows), 0)
    j = lax.broadcasted_iota(jnp.int32, (q_rows, q_rows), 1)
    earlier = jnp.where((along == along.T) & (i < j), 1.0, 0.0)
    rank = jnp.sum(earlier, axis=0, keepdims=True)
    slot = bucket * CAP + rank.astype(jnp.int32)
    slot_ref[...] = slot
    charge = jnp.broadcast_to(qcharge_ref[...].astype(F32), (META, q_rows)).astype(BF16)
    copies[2].wait()
    unit = unit_rows(q_ref[...])
    for k in range(4):
        plane = (me_ref[0] // PLANE) ^ k
        rel = (slot + (total - (plane * PLANE - 1) * CAP)) % total
        place = lax.broadcasted_iota(jnp.int32, (q_rows, q_rows), 0) == rel
        select = jnp.where(place, 1.0, 0.0).astype(BF16)
        rows = jnp.dot(select[:n_slots, :], unit, preferred_element_type=F32).astype(BF16)
        for n in range(width // 128):
            out_refs[k][n * n_slots : (n + 1) * n_slots, :] = rows[:, n * 128 : (n + 1) * 128]
        placed = lax.dot_general(
            charge, select, (((1,), (1,)), ((), ())), preferred_element_type=F32
        )
        out_refs[k][width // 128 * n_slots :, :] = placed.astype(BF16)
    copies[3].wait()
    lcharge = jnp.broadcast_to(lcharge_ref[...].astype(F32), lcharge_out.shape)
    lcharge_out[...] = lcharge.astype(BF16)


def unit_kernel(*refs):
    count = len(refs) // 2
    for source, target in zip(refs[:count], refs[count:]):
        for start in range(0, source.shape[0], 64):
            target[start : start + 64, :] = unit_rows(source[start : start + 64, :])


def pair_kernel(one_ref, other_ref, out_ref):
    line = lax.broadcasted_iota(jnp.int32, out_ref.shape, 0)
    one, other = one_ref[...].astype(F32), other_ref[...].astype(F32)
    out_ref[...] = jnp.where(line == 0, one, other).astype(BF16)


def score_kernel(turn, me_ref, *refs):
    lcharge_ref, lib_refs, out_refs = refs[4], refs[5:7], refs[7:11]
    q_refs = refs[3::-1]
    rows_ref, charge_ref = refs[11:]
    n_slots, seen = (PLANE + 2) * CAP, 3 * CAP
    for n, lib in enumerate(lib_refs):
        width = lib.shape[1]
        at = pl.multiple_of(((me_ref[0] % PLANE) ^ (turn ^ n)) * CAP, CAP)
        for k in range(4):
            for c in range(width // 128):
                rows_ref[k * seen : (k + 1) * seen, c * 128 : (c + 1) * 128] = q_refs[k][
                    pl.ds(pl.multiple_of(at + c * n_slots, CAP), seen), :
                ]
            if n == 0:
                line = q_refs[k][width // 128 * n_slots :, :].astype(F32)[0:1, :]
                charge_ref[k] = jnp.broadcast_to(line, (128, 128)).T
        lib_charge = lcharge_ref[...].astype(F32)[n : n + 1, :]
        products = lax.dot_general(
            rows_ref[...], lib[...], (((1,), (1,)), ((), ())), preferred_element_type=F32
        )
        for k in range(4):
            row_charge = charge_ref[k, pl.ds(at, seen), :][:, 0:1]
            kept = jnp.abs(row_charge - lib_charge) <= 2.0
            out_refs[k][n * seen : (n + 1) * seen, :] = jnp.where(
                kept, products[k * seen : (k + 1) * seen, :], 0.0
            ).astype(BF16)


def home_kernel(me_ref, slot_ref, *refs):
    near, far, out_ref, flat_ref = refs[3::-1], refs[7:3:-1], refs[8], refs[9]
    q_rows = slot_ref.shape[1]
    l_rows = near[0].shape[1]
    n_slab = 4 * PLANE
    total = n_slab * CAP
    slot = slot_ref[...]
    bucket, rank = slot // CAP, slot % CAP
    places = lax.broadcasted_iota(jnp.int32, (total, q_rows), 0)
    for unit in range(3):
        for m in range(n_slab):
            ref = (far if m & 2 else near)[m // PLANE]
            at = (m & 1) * 3 * CAP + (2 - unit) * CAP
            flat_ref[m * CAP : (m + 1) * CAP, :] = ref[at : at + CAP, :]
        slab = (bucket + (unit - 1 + n_slab)) % n_slab
        want = (slab ^ me_ref[0]) * CAP + rank
        select = jnp.where(places == want, 1.0, 0.0).T.astype(BF16)
        out_ref[:, unit * l_rows : (unit + 1) * l_rows] = jnp.dot(
            select, flat_ref[...], preferred_element_type=F32
        ).astype(BF16)


VMEM = pl.BlockSpec(memory_space=pltpu.VMEM)
SMEM = pl.BlockSpec(memory_space=pltpu.SMEM)
HBM = pl.BlockSpec(memory_space=pltpu.HBM)


MIB = 1024 * 1024


def kernel_call(body, outs, args, specs, scratch=(), limit=12 * MIB):
    return pl.pallas_call(
        body,
        out_shape=[jax.ShapeDtypeStruct(o.shape, o.dtype) for o in outs],
        in_specs=specs,
        out_specs=[VMEM] * len(outs),
        scratch_shapes=scratch,
        compiler_params=pltpu.CompilerParams(vmem_limit_bytes=limit),
        cost_estimate=pl.CostEstimate(flops=0, bytes_accessed=COST, transcendentals=0),
    )(*args)


def shape(*dims, dtype=BF16):
    return jax.ShapeDtypeStruct(dims, dtype)


def line_plan(queries, library, bucket, query_charge, library_charge):
    q_rows, width = queries.shape
    l_rows = library.shape[0]
    me = lax.axis_index("slab").astype(jnp.int32).reshape(1)
    n_slots, seen = (PLANE + 2) * CAP, 3 * CAP
    int32 = jnp.int32
    raw_y, raw_c = swapped(library, 2), swapped(library, 1)
    q0, q4, q8, q12, slot, charge = kernel_call(
        prep_kernel,
        [shape(width // 128 * n_slots + META, 128)] * 4
        + [shape(1, q_rows, dtype=int32), shape(META, l_rows)],
        [
            me,
            queries,
            bucket.reshape(1, q_rows),
            query_charge.reshape(1, q_rows),
            library_charge.reshape(1, l_rows),
        ],
        [SMEM] + [HBM] * 4,
        [
            pltpu.VMEM((q_rows, width), BF16),
            pltpu.VMEM((1, q_rows), int32),
            pltpu.VMEM((1, q_rows), int32),
            pltpu.VMEM((1, l_rows), int32),
            pltpu.SemaphoreType.DMA((4,)),
        ],
        limit=PREP_LIMIT,
    )
    q12, q8, q4 = swapped(q12, 12), swapped(q8, 8), swapped(q4, 4)
    lib = shape(l_rows, width)
    unit, unit_c = kernel_call(unit_kernel, [lib] * 2, [library, raw_c], [VMEM] * 2)
    charge_c = swapped(charge, 1)
    (near_charge,) = kernel_call(pair_kernel, [charge], [charge, charge_c], [VMEM] * 2)
    far_charge = swapped(near_charge, 2)
    scratch = [pltpu.VMEM((4 * seen, width), BF16), pltpu.VMEM((4, 128, 128), F32)]

    def scores(turn, charges, *units):
        blocks = kernel_call(
            functools.partial(score_kernel, turn),
            [shape(2 * seen, l_rows)] * 4,
            [me, q12, q8, q4, q0, charges, *units],
            [SMEM] + [VMEM] * 7,
            scratch,
        )
        return blocks

    def returned(blocks):
        far, middle, close = swapped(blocks[3], 12), swapped(blocks[2], 8), swapped(blocks[1], 4)
        return [far, middle, close, blocks[0]]

    near = list(scores(0, near_charge, unit, unit_c))
    raw_y, near[0] = lax.optimization_barrier((raw_y, near[0]))
    raw_d = swapped(raw_y, 1)
    near = returned(near)
    (unit_y,) = kernel_call(unit_kernel, [lib], [raw_y], [VMEM])
    (unit_d,) = kernel_call(unit_kernel, [lib], [raw_d], [VMEM])
    far = returned(scores(2, far_charge, unit_y, unit_d))
    (out,) = kernel_call(
        home_kernel,
        [shape(q_rows, 3 * l_rows)],
        [me, slot, *near, *far],
        [SMEM] + [VMEM] * 9,
        [pltpu.VMEM((4 * PLANE * CAP, l_rows), BF16)],
    )
    return out


def per_device(queries, library, bucket, query_charge, library_charge):
    n_slab = lax.axis_size("slab")
    q_rows, width = queries.shape
    fits = n_slab == 4 * PLANE and 2 * q_rows == n_slab * CAP and q_rows == 128
    plan = line_plan if fits and width % 256 == 0 and library.shape[0] <= width else general_plan
    return plan(queries, library, bucket, query_charge, library_charge)


def solution(mesh):
    placed = (
        P(("grp", "slab"), None),
        P(("grp", "slab"), None),
        P(("grp", "slab"), None),
        P(("grp", "slab")),
        P(("grp", "slab")),
    )
    return jax.shard_map(
        per_device, mesh=mesh, in_specs=placed, out_specs=P(("grp", "slab"), None), check_vma=False
    )
```

```python
import functools

import jax
import jax.numpy as jnp
from jax import lax
from jax.experimental import pallas as pl
from jax.experimental.pallas import tpu as pltpu
from jax.sharding import PartitionSpec as P

EPS = 1e-06
PLANE = 4
CAP = 16
META = 16
F32 = jnp.float32
BF16 = jnp.bfloat16


def passed_along(value, axis, steps):
    count = lax.axis_size(axis)
    pairs = [(source, (source + steps) % count) for source in range(count)]
    return lax.ppermute(value, axis, pairs)


def normalize(rows):
    values = rows.astype(F32)
    return (values * lax.rsqrt(jnp.sum(values * values, axis=-1, keepdims=True) + EPS)).astype(BF16)


def score_block(rows, row_charge, lib_rows, lib_charge):
    raw = lax.dot_general(rows, lib_rows, (((1,), (1,)), ((), ())), preferred_element_type=F32)
    keep = jnp.abs(row_charge.astype(F32)[:, None] - lib_charge.astype(F32)[None, :]) <= 2.0
    return jnp.where(keep, raw, 0.0).astype(BF16)


def selector(slot_ids, total):
    places = jnp.arange(total, dtype=jnp.int32)
    return (places[:, None] == slot_ids[None, :]).astype(BF16)


def pick_rows(select, flat):
    return lax.dot_general(
        select, flat, (((0,), (0,)), ((), ())), preferred_element_type=F32
    ).astype(BF16)


def place_rows(select, values):
    return jnp.dot(select, values, preferred_element_type=F32).astype(BF16)


def general_plan(queries, library, bucket, query_charge, library_charge):
    n_slab = lax.axis_size("slab")
    q_rows = queries.shape[0]
    width = queries.shape[1]
    cap = 2 * q_rows // n_slab
    query_unit = normalize(queries)
    library_unit = normalize(library)
    lib_charge = library_charge.astype(BF16)
    qcharge_col = query_charge.astype(BF16)[:, None]
    target = bucket[:, 0]
    positions = jnp.arange(q_rows, dtype=jnp.int32)
    earlier = (target[:, None] == target[None, :]) & (positions[None, :] < positions[:, None])
    rank = jnp.sum(earlier.astype(jnp.int32), axis=1)
    select_home = selector(target * cap + rank, n_slab * cap)
    outgoing = place_rows(select_home, query_unit).reshape(n_slab, cap, width)
    out_charge = place_rows(select_home, qcharge_col).reshape(n_slab, cap)
    below_rows, below_charge = passed_along((library_unit, lib_charge), "slab", 1)
    above_rows, above_charge = passed_along((library_unit, lib_charge), "slab", -1)
    rows = lax.all_to_all(outgoing, "slab", split_axis=0, concat_axis=0, tiled=True)
    charges = lax.all_to_all(out_charge, "slab", split_axis=0, concat_axis=0, tiled=True)
    count = rows.shape[1]
    flat = rows.reshape(n_slab * count, width)
    flat_charge = charges.reshape(n_slab * count)
    middle = score_block(flat, flat_charge, library_unit, lib_charge)
    lower = score_block(flat, flat_charge, below_rows, below_charge)
    upper = score_block(flat, flat_charge, above_rows, above_charge)
    joined = jnp.concatenate([lower, middle, upper], axis=1)
    joined = joined.reshape(n_slab, count, joined.shape[1])
    returned = lax.all_to_all(joined, "slab", split_axis=0, concat_axis=0, tiled=True)
    flat_back = returned.reshape(returned.shape[0] * returned.shape[1], returned.shape[2])
    return pick_rows(select_home, flat_back)


def swapped(value, mask):
    count = lax.axis_size("slab")
    return lax.ppermute(value, "slab", [(i, i ^ mask) for i in range(count)])


def unit_rows(values):
    values = values.astype(F32)
    return (values * lax.rsqrt(jnp.sum(values * values, axis=-1, keepdims=True) + EPS)).astype(BF16)


def slot_kernel(bucket_ref, qcharge_ref, lcharge_ref, slot_ref, qcharge_out, lcharge_out):
    q_rows = bucket_ref.shape[1]
    bucket = bucket_ref[...]
    along = jnp.broadcast_to(bucket.astype(F32), (q_rows, q_rows))
    i = lax.broadcasted_iota(jnp.int32, (q_rows, q_rows), 0)
    j = lax.broadcasted_iota(jnp.int32, (q_rows, q_rows), 1)
    earlier = jnp.where((along == along.T) & (i < j), 1.0, 0.0)
    rank = jnp.sum(earlier, axis=0, keepdims=True)
    slot_ref[...] = bucket * CAP + rank.astype(jnp.int32)
    for source, target in ((qcharge_ref, qcharge_out), (lcharge_ref, lcharge_out)):
        target[...] = jnp.broadcast_to(source[...].astype(F32), target.shape).astype(BF16)


def query_kernel(me_ref, slot_ref, charge_ref, q_ref, *out_refs):
    q_rows, width = q_ref.shape
    n_slots = (PLANE + 2) * CAP
    total = 4 * PLANE * CAP
    unit = unit_rows(q_ref[...])
    for k in range(4):
        plane = (me_ref[0] // PLANE) ^ k
        rel = (slot_ref[...] + (total - (plane * PLANE - 1) * CAP)) % total
        place = lax.broadcasted_iota(jnp.int32, (q_rows, q_rows), 0) == rel
        select = jnp.where(place, 1.0, 0.0).astype(BF16)
        rows = jnp.dot(select[:n_slots, :], unit, preferred_element_type=F32).astype(BF16)
        for n in range(width // 128):
            out_refs[k][n * n_slots : (n + 1) * n_slots, :] = rows[:, n * 128 : (n + 1) * 128]
        placed = lax.dot_general(
            charge_ref[...], select, (((1,), (1,)), ((), ())), preferred_element_type=F32
        )
        out_refs[k][width // 128 * n_slots :, :] = placed.astype(BF16)


def unit_kernel(*refs):
    count = len(refs) // 2
    for source, target in zip(refs[:count], refs[count:]):
        for start in range(0, source.shape[0], 64):
            target[start : start + 64, :] = unit_rows(source[start : start + 64, :])


def pair_kernel(one_ref, other_ref, out_ref):
    line = lax.broadcasted_iota(jnp.int32, out_ref.shape, 0)
    one, other = one_ref[...].astype(F32), other_ref[...].astype(F32)
    out_ref[...] = jnp.where(line == 0, one, other).astype(BF16)


def score_kernel(turn, me_ref, *refs):
    lcharge_ref, lib_refs, out_refs = refs[4], refs[5:7], refs[7:11]
    q_refs = [refs[at] for at in (3, 1, 0, 2)]
    rows_ref, charge_ref = refs[11:]
    n_slots, seen = (PLANE + 2) * CAP, 3 * CAP
    for n, lib in enumerate(lib_refs):
        width = lib.shape[1]
        at = pl.multiple_of(((me_ref[0] % PLANE) ^ (turn ^ n)) * CAP, CAP)
        for k in range(4):
            for c in range(width // 128):
                rows_ref[k * seen : (k + 1) * seen, c * 128 : (c + 1) * 128] = q_refs[k][
                    pl.ds(pl.multiple_of(at + c * n_slots, CAP), seen), :
                ]
            if n == 0:
                line = q_refs[k][width // 128 * n_slots :, :].astype(F32)[0:1, :]
                charge_ref[k] = jnp.broadcast_to(line, (128, 128)).T
        lib_charge = lcharge_ref[...].astype(F32)[n : n + 1, :]
        products = lax.dot_general(
            rows_ref[...], lib[...], (((1,), (1,)), ((), ())), preferred_element_type=F32
        )
        for k in range(4):
            row_charge = charge_ref[k, pl.ds(at, seen), :][:, 0:1]
            kept = jnp.abs(row_charge - lib_charge) <= 2.0
            out_refs[k][n * seen : (n + 1) * seen, :] = jnp.where(
                kept, products[k * seen : (k + 1) * seen, :], 0.0
            ).astype(BF16)


def home_kernel(me_ref, slot_ref, *refs):
    near, far = ([refs[first + at] for at in (3, 1, 0, 2)] for first in (0, 4))
    out_ref, flat_ref = refs[8], refs[9]
    q_rows = slot_ref.shape[1]
    l_rows = near[0].shape[1]
    n_slab = 4 * PLANE
    total = n_slab * CAP
    slot = slot_ref[...]
    bucket, rank = slot // CAP, slot % CAP
    places = lax.broadcasted_iota(jnp.int32, (total, q_rows), 0)
    for unit in range(3):
        for m in range(n_slab):
            ref = (far if m & 2 else near)[m // PLANE]
            at = (m & 1) * 3 * CAP + (2 - unit) * CAP
            flat_ref[m * CAP : (m + 1) * CAP, :] = ref[at : at + CAP, :]
        slab = (bucket + (unit - 1 + n_slab)) % n_slab
        want = (slab ^ me_ref[0]) * CAP + rank
        select = jnp.where(places == want, 1.0, 0.0).T.astype(BF16)
        out_ref[:, unit * l_rows : (unit + 1) * l_rows] = jnp.dot(
            select, flat_ref[...], preferred_element_type=F32
        ).astype(BF16)


VMEM = pl.BlockSpec(memory_space=pltpu.VMEM)
SMEM = pl.BlockSpec(memory_space=pltpu.SMEM)


MIB = 1024 * 1024


def kernel_call(body, outs, args, specs, scratch=(), cost=1):
    return pl.pallas_call(
        body,
        out_shape=[jax.ShapeDtypeStruct(o.shape, o.dtype) for o in outs],
        in_specs=specs,
        out_specs=[VMEM] * len(outs),
        scratch_shapes=scratch,
        compiler_params=pltpu.CompilerParams(vmem_limit_bytes=12 * MIB),
        cost_estimate=pl.CostEstimate(flops=0, bytes_accessed=cost, transcendentals=0),
    )(*args)


def shape(*dims, dtype=BF16):
    return jax.ShapeDtypeStruct(dims, dtype)


def line_plan(queries, library, bucket, query_charge, library_charge):
    q_rows, width = queries.shape
    l_rows = library.shape[0]
    me = lax.axis_index("slab").astype(jnp.int32).reshape(1)
    n_slots, seen = (PLANE + 2) * CAP, 3 * CAP
    int32 = jnp.int32
    raw_y, raw_c = swapped(library, 2), swapped(library, 1)
    slot, qcharge, charge = kernel_call(
        slot_kernel,
        [shape(1, q_rows, dtype=int32), shape(META, q_rows), shape(META, l_rows)],
        [x.reshape(1, -1) for x in (bucket, query_charge, library_charge)],
        [VMEM] * 3,
        cost=1,
    )
    q0, q4, q8, q12 = kernel_call(
        query_kernel,
        [shape(width // 128 * n_slots + META, 128)] * 4,
        [me, slot, qcharge, queries],
        [SMEM] + [VMEM] * 3,
    )
    q12, q8, q4 = swapped(q12, 12), swapped(q8, 8), swapped(q4, 4)
    lib = shape(l_rows, width)
    unit, unit_c = kernel_call(unit_kernel, [lib] * 2, [library, raw_c], [VMEM] * 2)
    charge_c = swapped(charge, 1)
    (near_charge,) = kernel_call(pair_kernel, [charge], [charge, charge_c], [VMEM] * 2)
    far_charge = swapped(near_charge, 2)
    scratch = [pltpu.VMEM((4 * seen, width), BF16), pltpu.VMEM((4, 128, 128), F32)]

    def scores(turn, charges, *units):
        blocks = kernel_call(
            functools.partial(score_kernel, turn),
            [shape(2 * seen, l_rows)] * 4,
            [me, q8, q4, q12, q0, charges, *units],
            [SMEM] + [VMEM] * 7,
            scratch,
        )
        return blocks

    def returned(blocks):
        far, middle, close = swapped(blocks[3], 12), swapped(blocks[2], 8), swapped(blocks[1], 4)
        return [middle, close, far, blocks[0]]

    near = list(scores(0, near_charge, unit, unit_c))
    raw_y, near[0] = lax.optimization_barrier((raw_y, near[0]))
    raw_d = swapped(raw_y, 1)
    near = returned(near)
    (unit_y,) = kernel_call(unit_kernel, [lib], [raw_y], [VMEM])
    (unit_d,) = kernel_call(unit_kernel, [lib], [raw_d], [VMEM])
    far = returned(scores(2, far_charge, unit_y, unit_d))
    (out,) = kernel_call(
        home_kernel,
        [shape(q_rows, 3 * l_rows)],
        [me, slot, *near, *far],
        [SMEM] + [VMEM] * 9,
        [pltpu.VMEM((4 * PLANE * CAP, l_rows), BF16)],
    )
    return out


def per_device(queries, library, bucket, query_charge, library_charge):
    n_slab = lax.axis_size("slab")
    q_rows, width = queries.shape
    fits = n_slab == 4 * PLANE and 2 * q_rows == n_slab * CAP and q_rows == 128
    plan = line_plan if fits and width % 256 == 0 and library.shape[0] <= width else general_plan
    return plan(queries, library, bucket, query_charge, library_charge)


def solution(mesh):
    placed = (
        P(("grp", "slab"), None),
        P(("grp", "slab"), None),
        P(("grp", "slab"), None),
        P(("grp", "slab")),
        P(("grp", "slab")),
    )
    return jax.shard_map(
        per_device, mesh=mesh, in_specs=placed, out_specs=P(("grp", "slab"), None), check_vma=False
    )
```

```python
import functools

import jax
import jax.numpy as jnp
from jax import lax
from jax.experimental import pallas as pl
from jax.experimental.pallas import tpu as pltpu
from jax.sharding import PartitionSpec as P

EPS = 1e-06
PLANE = 4
CAP = 16
META = 16
F32 = jnp.float32
BF16 = jnp.bfloat16


def passed_along(value, axis, steps):
    count = lax.axis_size(axis)
    pairs = [(source, (source + steps) % count) for source in range(count)]
    return lax.ppermute(value, axis, pairs)


def normalize(rows):
    values = rows.astype(F32)
    return (values * lax.rsqrt(jnp.sum(values * values, axis=-1, keepdims=True) + EPS)).astype(BF16)


def score_block(rows, row_charge, lib_rows, lib_charge):
    raw = lax.dot_general(rows, lib_rows, (((1,), (1,)), ((), ())), preferred_element_type=F32)
    keep = jnp.abs(row_charge.astype(F32)[:, None] - lib_charge.astype(F32)[None, :]) <= 2.0
    return jnp.where(keep, raw, 0.0).astype(BF16)


def selector(slot_ids, total):
    places = jnp.arange(total, dtype=jnp.int32)
    return (places[:, None] == slot_ids[None, :]).astype(BF16)


def pick_rows(select, flat):
    return lax.dot_general(
        select, flat, (((0,), (0,)), ((), ())), preferred_element_type=F32
    ).astype(BF16)


def place_rows(select, values):
    return jnp.dot(select, values, preferred_element_type=F32).astype(BF16)


def general_plan(queries, library, bucket, query_charge, library_charge):
    n_slab = lax.axis_size("slab")
    q_rows = queries.shape[0]
    width = queries.shape[1]
    cap = 2 * q_rows // n_slab
    query_unit = normalize(queries)
    library_unit = normalize(library)
    lib_charge = library_charge.astype(BF16)
    qcharge_col = query_charge.astype(BF16)[:, None]
    target = bucket[:, 0]
    positions = jnp.arange(q_rows, dtype=jnp.int32)
    earlier = (target[:, None] == target[None, :]) & (positions[None, :] < positions[:, None])
    rank = jnp.sum(earlier.astype(jnp.int32), axis=1)
    select_home = selector(target * cap + rank, n_slab * cap)
    outgoing = place_rows(select_home, query_unit).reshape(n_slab, cap, width)
    out_charge = place_rows(select_home, qcharge_col).reshape(n_slab, cap)
    below_rows, below_charge = passed_along((library_unit, lib_charge), "slab", 1)
    above_rows, above_charge = passed_along((library_unit, lib_charge), "slab", -1)
    rows = lax.all_to_all(outgoing, "slab", split_axis=0, concat_axis=0, tiled=True)
    charges = lax.all_to_all(out_charge, "slab", split_axis=0, concat_axis=0, tiled=True)
    count = rows.shape[1]
    flat = rows.reshape(n_slab * count, width)
    flat_charge = charges.reshape(n_slab * count)
    middle = score_block(flat, flat_charge, library_unit, lib_charge)
    lower = score_block(flat, flat_charge, below_rows, below_charge)
    upper = score_block(flat, flat_charge, above_rows, above_charge)
    joined = jnp.concatenate([lower, middle, upper], axis=1)
    joined = joined.reshape(n_slab, count, joined.shape[1])
    returned = lax.all_to_all(joined, "slab", split_axis=0, concat_axis=0, tiled=True)
    flat_back = returned.reshape(returned.shape[0] * returned.shape[1], returned.shape[2])
    return pick_rows(select_home, flat_back)


def swapped(value, mask):
    count = lax.axis_size("slab")
    return lax.ppermute(value, "slab", [(i, i ^ mask) for i in range(count)])


def unit_rows(values):
    values = values.astype(F32)
    return (values * lax.rsqrt(jnp.sum(values * values, axis=-1, keepdims=True) + EPS)).astype(BF16)


def slot_kernel(bucket_ref, qcharge_ref, lcharge_ref, slot_ref, qcharge_out, lcharge_out):
    q_rows = bucket_ref.shape[1]
    bucket = bucket_ref[...]
    along = jnp.broadcast_to(bucket.astype(F32), (q_rows, q_rows))
    i = lax.broadcasted_iota(jnp.int32, (q_rows, q_rows), 0)
    j = lax.broadcasted_iota(jnp.int32, (q_rows, q_rows), 1)
    earlier = jnp.where((along == along.T) & (i < j), 1.0, 0.0)
    rank = jnp.sum(earlier, axis=0, keepdims=True)
    slot_ref[...] = bucket * CAP + rank.astype(jnp.int32)
    for source, target in ((qcharge_ref, qcharge_out), (lcharge_ref, lcharge_out)):
        target[...] = jnp.broadcast_to(source[...].astype(F32), target.shape).astype(BF16)


def query_kernel(me_ref, slot_ref, charge_ref, q_ref, *out_refs):
    q_rows, width = q_ref.shape
    n_slots = (PLANE + 2) * CAP
    total = 4 * PLANE * CAP
    unit = unit_rows(q_ref[...])
    for k in range(4):
        plane = (me_ref[0] // PLANE) ^ k
        rel = (slot_ref[...] + (total - (plane * PLANE - 1) * CAP)) % total
        place = lax.broadcasted_iota(jnp.int32, (q_rows, q_rows), 0) == rel
        select = jnp.where(place, 1.0, 0.0).astype(BF16)
        rows = jnp.dot(select[:n_slots, :], unit, preferred_element_type=F32).astype(BF16)
        for n in range(width // 128):
            out_refs[k][n * n_slots : (n + 1) * n_slots, :] = rows[:, n * 128 : (n + 1) * 128]
        placed = lax.dot_general(
            charge_ref[...], select, (((1,), (1,)), ((), ())), preferred_element_type=F32
        )
        out_refs[k][width // 128 * n_slots :, :] = placed.astype(BF16)


def unit_kernel(*refs):
    count = len(refs) // 2
    for source, target in zip(refs[:count], refs[count:]):
        for start in range(0, source.shape[0], 64):
            target[start : start + 64, :] = unit_rows(source[start : start + 64, :])


def pair_kernel(one_ref, other_ref, out_ref):
    line = lax.broadcasted_iota(jnp.int32, out_ref.shape, 0)
    one, other = one_ref[...].astype(F32), other_ref[...].astype(F32)
    out_ref[...] = jnp.where(line == 0, one, other).astype(BF16)


def score_kernel(count, turn, me_ref, *refs):
    q_refs, refs = refs[:count], refs[count:]
    lcharge_ref, lib_refs, out_refs = refs[0], refs[1:3], refs[3 : 3 + count]
    rows_ref, charge_ref = refs[3 + count :]
    n_slots, seen = (PLANE + 2) * CAP, 3 * CAP
    for n, lib in enumerate(lib_refs):
        width = lib.shape[1]
        at = pl.multiple_of(((me_ref[0] % PLANE) ^ (turn ^ n)) * CAP, CAP)
        for k in range(count):
            for c in range(width // 128):
                rows_ref[k * seen : (k + 1) * seen, c * 128 : (c + 1) * 128] = q_refs[k][
                    pl.ds(pl.multiple_of(at + c * n_slots, CAP), seen), :
                ]
            if n == 0:
                line = q_refs[k][width // 128 * n_slots :, :].astype(F32)[0:1, :]
                charge_ref[k] = jnp.broadcast_to(line, (128, 128)).T
        lib_charge = lcharge_ref[...].astype(F32)[n : n + 1, :]
        products = lax.dot_general(
            rows_ref[...], lib[...], (((1,), (1,)), ((), ())), preferred_element_type=F32
        )
        for k in range(count):
            row_charge = charge_ref[k, pl.ds(at, seen), :][:, 0:1]
            kept = jnp.abs(row_charge - lib_charge) <= 2.0
            out_refs[k][n * seen : (n + 1) * seen, :] = jnp.where(
                kept, products[k * seen : (k + 1) * seen, :], 0.0
            ).astype(BF16)


def home_kernel(me_ref, slot_ref, *refs):
    near = [refs[at] for at in (0, 1, 2, 3)]
    far = [refs[4 + at] for at in (3, 1, 0, 2)]
    out_ref, flat_ref = refs[8], refs[9]
    q_rows = slot_ref.shape[1]
    l_rows = near[0].shape[1]
    n_slab = 4 * PLANE
    total = n_slab * CAP
    slot = slot_ref[...]
    bucket, rank = slot // CAP, slot % CAP
    places = lax.broadcasted_iota(jnp.int32, (total, q_rows), 0)
    for unit in range(3):
        for m in range(n_slab):
            ref = (far if m & 2 else near)[m // PLANE]
            at = (m & 1) * 3 * CAP + (2 - unit) * CAP
            flat_ref[m * CAP : (m + 1) * CAP, :] = ref[at : at + CAP, :]
        slab = (bucket + (unit - 1 + n_slab)) % n_slab
        want = (slab ^ me_ref[0]) * CAP + rank
        select = jnp.where(places == want, 1.0, 0.0).T.astype(BF16)
        out_ref[:, unit * l_rows : (unit + 1) * l_rows] = jnp.dot(
            select, flat_ref[...], preferred_element_type=F32
        ).astype(BF16)


VMEM = pl.BlockSpec(memory_space=pltpu.VMEM)
SMEM = pl.BlockSpec(memory_space=pltpu.SMEM)


MIB = 1024 * 1024


def kernel_call(body, outs, args, specs, scratch=(), cost=1):
    return pl.pallas_call(
        body,
        out_shape=[jax.ShapeDtypeStruct(o.shape, o.dtype) for o in outs],
        in_specs=specs,
        out_specs=[VMEM] * len(outs),
        scratch_shapes=scratch,
        compiler_params=pltpu.CompilerParams(vmem_limit_bytes=12 * MIB),
        cost_estimate=pl.CostEstimate(flops=0, bytes_accessed=cost, transcendentals=0),
    )(*args)


def shape(*dims, dtype=BF16):
    return jax.ShapeDtypeStruct(dims, dtype)


def line_plan(queries, library, bucket, query_charge, library_charge):
    q_rows, width = queries.shape
    l_rows = library.shape[0]
    me = lax.axis_index("slab").astype(jnp.int32).reshape(1)
    n_slots, seen = (PLANE + 2) * CAP, 3 * CAP
    int32 = jnp.int32
    raw_y, raw_c = swapped(library, 2), swapped(library, 1)
    slot, qcharge, charge = kernel_call(
        slot_kernel,
        [shape(1, q_rows, dtype=int32), shape(META, q_rows), shape(META, l_rows)],
        [x.reshape(1, -1) for x in (bucket, query_charge, library_charge)],
        [VMEM] * 3,
        cost=1,
    )
    q0, q4, q8, q12 = kernel_call(
        query_kernel,
        [shape(width // 128 * n_slots + META, 128)] * 4,
        [me, slot, qcharge, queries],
        [SMEM] + [VMEM] * 3,
    )
    q12, q8, q4 = swapped(q12, 12), swapped(q8, 8), swapped(q4, 4)
    lib = shape(l_rows, width)
    unit, unit_c = kernel_call(unit_kernel, [lib] * 2, [library, raw_c], [VMEM] * 2)
    charge_c = swapped(charge, 1)
    (near_charge,) = kernel_call(pair_kernel, [charge], [charge, charge_c], [VMEM] * 2)
    far_charge = swapped(near_charge, 2)

    def scores(turn, q_blocks, *parts):
        count = len(q_blocks)
        return kernel_call(
            functools.partial(score_kernel, count, turn),
            [shape(2 * seen, l_rows)] * count,
            [me, *q_blocks, *parts],
            [SMEM] + [VMEM] * (count + len(parts)),
            [pltpu.VMEM((count * seen, width), BF16), pltpu.VMEM((count, 128, 128), F32)],
        )

    near8, near4, near0 = scores(0, [q8, q4, q0], near_charge, unit, unit_c)
    near8, near4 = swapped(near8, 8), swapped(near4, 4)
    raw_y, q12, near8, near4, far_charge = lax.optimization_barrier(
        (raw_y, q12, near8, near4, far_charge)
    )
    raw_d = swapped(raw_y, 1)
    (near12,) = scores(0, [q12], near_charge, unit, unit_c)
    near12 = swapped(near12, 12)
    (unit_y,) = kernel_call(unit_kernel, [lib], [raw_y], [VMEM])
    (unit_d,) = kernel_call(unit_kernel, [lib], [raw_d], [VMEM])
    far8, far4, far12, far0 = scores(2, [q8, q4, q12, q0], far_charge, unit_y, unit_d)
    far8, far4, far12 = swapped(far8, 8), swapped(far4, 4), swapped(far12, 12)
    near, far = [near0, near4, near8, near12], [far8, far4, far12, far0]
    (out,) = kernel_call(
        home_kernel,
        [shape(q_rows, 3 * l_rows)],
        [me, slot, *near, *far],
        [SMEM] + [VMEM] * 9,
        [pltpu.VMEM((4 * PLANE * CAP, l_rows), BF16)],
    )
    return out


def per_device(queries, library, bucket, query_charge, library_charge):
    n_slab = lax.axis_size("slab")
    q_rows, width = queries.shape
    fits = n_slab == 4 * PLANE and 2 * q_rows == n_slab * CAP and q_rows == 128
    plan = line_plan if fits and width % 256 == 0 and library.shape[0] <= width else general_plan
    return plan(queries, library, bucket, query_charge, library_charge)


def solution(mesh):
    placed = (
        P(("grp", "slab"), None),
        P(("grp", "slab"), None),
        P(("grp", "slab"), None),
        P(("grp", "slab")),
        P(("grp", "slab")),
    )
    return jax.shard_map(
        per_device, mesh=mesh, in_specs=placed, out_specs=P(("grp", "slab"), None), check_vma=False
    )
```

```python
import functools

import jax
import jax.numpy as jnp
from jax import lax
from jax.experimental import pallas as pl
from jax.experimental.pallas import tpu as pltpu
from jax.sharding import PartitionSpec as P

EPS = 1e-06
PLANE = 4
CAP = 16
META = 16
F32 = jnp.float32
BF16 = jnp.bfloat16


def passed_along(value, axis, steps):
    count = lax.axis_size(axis)
    pairs = [(source, (source + steps) % count) for source in range(count)]
    return lax.ppermute(value, axis, pairs)


def normalize(rows):
    values = rows.astype(F32)
    return (values * lax.rsqrt(jnp.sum(values * values, axis=-1, keepdims=True) + EPS)).astype(BF16)


def score_block(rows, row_charge, lib_rows, lib_charge):
    raw = lax.dot_general(rows, lib_rows, (((1,), (1,)), ((), ())), preferred_element_type=F32)
    keep = jnp.abs(row_charge.astype(F32)[:, None] - lib_charge.astype(F32)[None, :]) <= 2.0
    return jnp.where(keep, raw, 0.0).astype(BF16)


def selector(slot_ids, total):
    places = jnp.arange(total, dtype=jnp.int32)
    return (places[:, None] == slot_ids[None, :]).astype(BF16)


def pick_rows(select, flat):
    return lax.dot_general(
        select, flat, (((0,), (0,)), ((), ())), preferred_element_type=F32
    ).astype(BF16)


def place_rows(select, values):
    return jnp.dot(select, values, preferred_element_type=F32).astype(BF16)


def general_plan(queries, library, bucket, query_charge, library_charge):
    n_slab = lax.axis_size("slab")
    q_rows = queries.shape[0]
    width = queries.shape[1]
    cap = 2 * q_rows // n_slab
    query_unit = normalize(queries)
    library_unit = normalize(library)
    lib_charge = library_charge.astype(BF16)
    qcharge_col = query_charge.astype(BF16)[:, None]
    target = bucket[:, 0]
    positions = jnp.arange(q_rows, dtype=jnp.int32)
    earlier = (target[:, None] == target[None, :]) & (positions[None, :] < positions[:, None])
    rank = jnp.sum(earlier.astype(jnp.int32), axis=1)
    select_home = selector(target * cap + rank, n_slab * cap)
    outgoing = place_rows(select_home, query_unit).reshape(n_slab, cap, width)
    out_charge = place_rows(select_home, qcharge_col).reshape(n_slab, cap)
    below_rows, below_charge = passed_along((library_unit, lib_charge), "slab", 1)
    above_rows, above_charge = passed_along((library_unit, lib_charge), "slab", -1)
    rows = lax.all_to_all(outgoing, "slab", split_axis=0, concat_axis=0, tiled=True)
    charges = lax.all_to_all(out_charge, "slab", split_axis=0, concat_axis=0, tiled=True)
    count = rows.shape[1]
    flat = rows.reshape(n_slab * count, width)
    flat_charge = charges.reshape(n_slab * count)
    middle = score_block(flat, flat_charge, library_unit, lib_charge)
    lower = score_block(flat, flat_charge, below_rows, below_charge)
    upper = score_block(flat, flat_charge, above_rows, above_charge)
    joined = jnp.concatenate([lower, middle, upper], axis=1)
    joined = joined.reshape(n_slab, count, joined.shape[1])
    returned = lax.all_to_all(joined, "slab", split_axis=0, concat_axis=0, tiled=True)
    flat_back = returned.reshape(returned.shape[0] * returned.shape[1], returned.shape[2])
    return pick_rows(select_home, flat_back)


def swapped(value, mask):
    count = lax.axis_size("slab")
    return lax.ppermute(value, "slab", [(i, i ^ mask) for i in range(count)])


def unit_rows(values):
    values = values.astype(F32)
    return (values * lax.rsqrt(jnp.sum(values * values, axis=-1, keepdims=True) + EPS)).astype(BF16)


def slot_kernel(bucket_ref, qcharge_ref, lcharge_ref, slot_ref, qcharge_out, lcharge_out):
    q_rows = bucket_ref.shape[1]
    bucket = bucket_ref[...]
    along = jnp.broadcast_to(bucket.astype(F32), (q_rows, q_rows))
    i = lax.broadcasted_iota(jnp.int32, (q_rows, q_rows), 0)
    j = lax.broadcasted_iota(jnp.int32, (q_rows, q_rows), 1)
    earlier = jnp.where((along == along.T) & (i < j), 1.0, 0.0)
    rank = jnp.sum(earlier, axis=0, keepdims=True)
    slot_ref[...] = bucket * CAP + rank.astype(jnp.int32)
    for source, target in ((qcharge_ref, qcharge_out), (lcharge_ref, lcharge_out)):
        target[...] = jnp.broadcast_to(source[...].astype(F32), target.shape).astype(BF16)


def query_kernel(me_ref, slot_ref, charge_ref, q_ref, *out_refs):
    q_rows, width = q_ref.shape
    n_slots = (PLANE + 2) * CAP
    total = 4 * PLANE * CAP
    unit = unit_rows(q_ref[...])
    for k in range(4):
        plane = (me_ref[0] // PLANE) ^ k
        count = n_slots if k < 3 else n_slots - 2 * CAP
        skip = plane % 2 * (2 * CAP) if k == 3 else 0
        rel = (slot_ref[...] + (total - (plane * PLANE - 1) * CAP)) % total - skip
        place = lax.broadcasted_iota(jnp.int32, (q_rows, q_rows), 0) == rel
        select = jnp.where(place, 1.0, 0.0).astype(BF16)
        rows = jnp.dot(select[:count, :], unit, preferred_element_type=F32).astype(BF16)
        for n in range(width // 128):
            out_refs[k][n * count : (n + 1) * count, :] = rows[:, n * 128 : (n + 1) * 128]
        placed = lax.dot_general(
            charge_ref[...], select, (((1,), (1,)), ((), ())), preferred_element_type=F32
        )
        out_refs[k][width // 128 * count :, :] = placed.astype(BF16)


def unit_kernel(*refs):
    count = len(refs) // 2
    for source, target in zip(refs[:count], refs[count:]):
        for start in range(0, source.shape[0], 64):
            target[start : start + 64, :] = unit_rows(source[start : start + 64, :])


def pair_kernel(one_ref, other_ref, out_ref):
    line = lax.broadcasted_iota(jnp.int32, out_ref.shape, 0)
    one, other = one_ref[...].astype(F32), other_ref[...].astype(F32)
    out_ref[...] = jnp.where(line == 0, one, other).astype(BF16)


def score_kernel(count, turn, me_ref, *refs):
    q_refs, refs = refs[:count], refs[count:]
    lcharge_ref, lib_refs, out_refs = refs[0], refs[1:3], refs[3 : 3 + count]
    rows_ref, charge_ref = refs[3 + count :]
    n_slots, seen = (PLANE + 2) * CAP, 3 * CAP
    for n, lib in enumerate(lib_refs):
        width = lib.shape[1]
        at = pl.multiple_of(((me_ref[0] % PLANE) ^ (turn ^ n)) * CAP, CAP)
        for k in range(count):
            for c in range(width // 128):
                rows_ref[k * seen : (k + 1) * seen, c * 128 : (c + 1) * 128] = q_refs[k][
                    pl.ds(pl.multiple_of(at + c * n_slots, CAP), seen), :
                ]
            if n == 0:
                line = q_refs[k][width // 128 * n_slots :, :].astype(F32)[0:1, :]
                charge_ref[k] = jnp.broadcast_to(line, (128, 128)).T
        lib_charge = lcharge_ref[...].astype(F32)[n : n + 1, :]
        products = lax.dot_general(
            rows_ref[...], lib[...], (((1,), (1,)), ((), ())), preferred_element_type=F32
        )
        for k in range(count):
            row_charge = charge_ref[k, pl.ds(at, seen), :][:, 0:1]
            kept = jnp.abs(row_charge - lib_charge) <= 2.0
            out_refs[k][n * seen : (n + 1) * seen, :] = jnp.where(
                kept, products[k * seen : (k + 1) * seen, :], 0.0
            ).astype(BF16)


def first_kernel(me_ref, *refs):
    score_kernel(3, 0, me_ref, *refs[:9], *refs[10:])
    q_ref, out_ref = refs[0], refs[9]
    n_slots, shared = (PLANE + 2) * CAP, 2 * CAP
    count = (q_ref.shape[0] - META) // n_slots
    at = (1 - me_ref[0] // PLANE % 2) * (n_slots - shared)
    wide = out_ref.shape[1] // 128
    for n in range(count):
        row, column = n // wide * shared, n % wide * 128
        out_ref[row : row + shared, column : column + 128] = q_ref[
            pl.ds(pl.multiple_of(at + n * n_slots, CAP), shared), :
        ]
    row = count // wide * shared
    out_ref[row:, :] = jnp.zeros((META, out_ref.shape[1]), BF16)
    out_ref[row:, :128] = q_ref[count * n_slots :, :]


def second_kernel(me_ref, q_ref, passed_ref, *refs):
    charge_refs, lib_refs, out_ref, block_ref = refs[0], refs[1:3], refs[3], refs[4]
    rows_ref, charge_ref, column_ref = refs[5:]
    n_slots, shared = (PLANE + 2) * CAP, 2 * CAP
    part = n_slots - shared
    count = (q_ref.shape[0] - META) // part
    wide = passed_ref.shape[1] // 128
    odd = me_ref[0] // PLANE % 2
    own_at, passed_at = odd * shared, (1 - odd) * part
    for n in range(count):
        row, column = n // wide * shared, n % wide * 128
        block_ref[pl.ds(pl.multiple_of(n * n_slots + own_at, CAP), part), :] = q_ref[
            n * part : (n + 1) * part, :
        ]
        block_ref[pl.ds(pl.multiple_of(n * n_slots + passed_at, CAP), shared), :] = passed_ref[
            row : row + shared, column : column + 128
        ]
    row = count // wide * shared
    own_line = q_ref[count * part :, :].astype(F32)[0:1, :]
    passed_line = passed_ref[row:, :128].astype(F32)[0:1, :]
    column_ref[0] = jnp.broadcast_to(passed_line, (128, 128)).T
    column_ref[1] = jnp.broadcast_to(own_line, (128, 128)).T
    column_ref[2] = jnp.zeros((128, 128), F32)
    column_ref[2, pl.ds(pl.multiple_of(own_at, CAP), part), :] = column_ref[1, :part, :]
    column_ref[2, pl.ds(pl.multiple_of(passed_at, CAP), shared), :] = column_ref[
        0, pl.ds(pl.multiple_of(odd * part, CAP), shared), :
    ]
    block_ref[count * n_slots :, :] = column_ref[2].T[:META, :].astype(BF16)
    score_kernel(1, 0, me_ref, block_ref, charge_refs, *lib_refs, out_ref, rows_ref, charge_ref)


def home_kernel(me_ref, slot_ref, *refs):
    near8, near12, near4, near0, far8, far4, far12, far0, out_ref, flat_ref = refs
    near = [near0, near4, near8, near12]
    far = [far0, far4, far8, far12]
    q_rows = slot_ref.shape[1]
    l_rows = near0.shape[1]
    n_slab = 4 * PLANE
    total = n_slab * CAP
    slot = slot_ref[...]
    bucket, rank = slot // CAP, slot % CAP
    places = lax.broadcasted_iota(jnp.int32, (total, q_rows), 0)
    for unit in range(3):
        for m in range(n_slab):
            ref = (far if m & 2 else near)[m // PLANE]
            at = (m & 1) * 3 * CAP + (2 - unit) * CAP
            flat_ref[m * CAP : (m + 1) * CAP, :] = ref[at : at + CAP, :]
        slab = (bucket + (unit - 1 + n_slab)) % n_slab
        want = (slab ^ me_ref[0]) * CAP + rank
        select = jnp.where(places == want, 1.0, 0.0).T.astype(BF16)
        out_ref[:, unit * l_rows : (unit + 1) * l_rows] = jnp.dot(
            select, flat_ref[...], preferred_element_type=F32
        ).astype(BF16)


VMEM = pl.BlockSpec(memory_space=pltpu.VMEM)
SMEM = pl.BlockSpec(memory_space=pltpu.SMEM)


MIB = 1024 * 1024


def kernel_call(body, outs, args, specs, scratch=(), cost=1):
    return pl.pallas_call(
        body,
        out_shape=[jax.ShapeDtypeStruct(o.shape, o.dtype) for o in outs],
        in_specs=specs,
        out_specs=[VMEM] * len(outs),
        scratch_shapes=scratch,
        compiler_params=pltpu.CompilerParams(vmem_limit_bytes=12 * MIB),
        cost_estimate=pl.CostEstimate(flops=0, bytes_accessed=cost, transcendentals=0),
    )(*args)


def shape(*dims, dtype=BF16):
    return jax.ShapeDtypeStruct(dims, dtype)


def line_plan(queries, library, bucket, query_charge, library_charge):
    q_rows, width = queries.shape
    l_rows = library.shape[0]
    me = lax.axis_index("slab").astype(jnp.int32).reshape(1)
    n_slots, seen = (PLANE + 2) * CAP, 3 * CAP
    int32 = jnp.int32
    raw_y, raw_c = swapped(library, 2), swapped(library, 1)
    slot, qcharge, charge = kernel_call(
        slot_kernel,
        [shape(1, q_rows, dtype=int32), shape(META, q_rows), shape(META, l_rows)],
        [x.reshape(1, -1) for x in (bucket, query_charge, library_charge)],
        [VMEM] * 3,
        cost=1,
    )
    slots_shape = shape(width // 128 * n_slots + META, 128)
    q0, q4, q8, q12 = kernel_call(
        query_kernel,
        [slots_shape] * 3 + [shape(width // 128 * (n_slots - 2 * CAP) + META, 128)],
        [me, slot, qcharge, queries],
        [SMEM] + [VMEM] * 3,
    )
    q12, q8, q4 = swapped(q12, 12), swapped(q8, 8), swapped(q4, 4)
    lib = shape(l_rows, width)
    unit, unit_c = kernel_call(unit_kernel, [lib] * 2, [library, raw_c], [VMEM] * 2)
    charge_c = swapped(charge, 1)
    (near_charge,) = kernel_call(pair_kernel, [charge], [charge, charge_c], [VMEM] * 2)
    far_charge = swapped(near_charge, 2)

    block = shape(2 * seen, l_rows)
    shared_rows = width // l_rows * 2 * CAP + META
    first = [q8, q4, q0, near_charge, unit, unit_c]
    near8, near4, near0, passed = kernel_call(
        first_kernel,
        [block] * 3 + [shape(shared_rows, l_rows)],
        [me, *first],
        [SMEM] + [VMEM] * len(first),
        [pltpu.VMEM((3 * seen, width), BF16), pltpu.VMEM((3, 128, 128), F32)],
    )
    near8, passed = swapped(near8, 8), swapped(passed, 4)
    raw_y, q12, near8, near4, passed, far_charge = lax.optimization_barrier(
        (raw_y, q12, near8, near4, passed, far_charge)
    )
    raw_d = swapped(raw_y, 1)
    near12, q12 = kernel_call(
        second_kernel,
        [block, slots_shape],
        [me, q12, passed, near_charge, unit, unit_c],
        [SMEM] + [VMEM] * 5,
        [
            pltpu.VMEM((seen, width), BF16),
            pltpu.VMEM((1, 128, 128), F32),
            pltpu.VMEM((3, 128, 128), F32),
        ],
    )
    near12, near4 = swapped(near12, 12), swapped(near4, 4)
    (unit_y,) = kernel_call(unit_kernel, [lib], [raw_y], [VMEM])
    (unit_d,) = kernel_call(unit_kernel, [lib], [raw_d], [VMEM])
    far8, far4, far12, far0 = kernel_call(
        functools.partial(score_kernel, 4, 2),
        [block] * 4,
        [me, q8, q4, q12, q0, far_charge, unit_y, unit_d],
        [SMEM] + [VMEM] * 7,
        [pltpu.VMEM((4 * seen, width), BF16), pltpu.VMEM((4, 128, 128), F32)],
    )
    far8, far4, far12 = swapped(far8, 8), swapped(far4, 4), swapped(far12, 12)
    (out,) = kernel_call(
        home_kernel,
        [shape(q_rows, 3 * l_rows)],
        [me, slot, near8, near12, near4, near0, far8, far4, far12, far0],
        [SMEM] + [VMEM] * 9,
        [pltpu.VMEM((4 * PLANE * CAP, l_rows), BF16)],
    )
    return out


def per_device(queries, library, bucket, query_charge, library_charge):
    n_slab = lax.axis_size("slab")
    q_rows, width = queries.shape
    fits = n_slab == 4 * PLANE and 2 * q_rows == n_slab * CAP and q_rows == 128
    plan = line_plan if fits and width % 256 == 0 and width % (2 * library.shape[0]) == 0 else general_plan
    return plan(queries, library, bucket, query_charge, library_charge)


def solution(mesh):
    placed = (
        P(("grp", "slab"), None),
        P(("grp", "slab"), None),
        P(("grp", "slab"), None),
        P(("grp", "slab")),
        P(("grp", "slab")),
    )
    return jax.shard_map(
        per_device, mesh=mesh, in_specs=placed, out_specs=P(("grp", "slab"), None), check_vma=False
    )
```

```python
import functools

import jax
import jax.numpy as jnp
from jax import lax
from jax.experimental import pallas as pl
from jax.experimental.pallas import tpu as pltpu
from jax.sharding import PartitionSpec as P

EPS = 1e-06
PLANE = 4
CAP = 16
META = 16
F32 = jnp.float32
BF16 = jnp.bfloat16


def passed_along(value, axis, steps):
    count = lax.axis_size(axis)
    pairs = [(source, (source + steps) % count) for source in range(count)]
    return lax.ppermute(value, axis, pairs)


def normalize(rows):
    values = rows.astype(F32)
    return (values * lax.rsqrt(jnp.sum(values * values, axis=-1, keepdims=True) + EPS)).astype(BF16)


def score_block(rows, row_charge, lib_rows, lib_charge):
    raw = lax.dot_general(rows, lib_rows, (((1,), (1,)), ((), ())), preferred_element_type=F32)
    keep = jnp.abs(row_charge.astype(F32)[:, None] - lib_charge.astype(F32)[None, :]) <= 2.0
    return jnp.where(keep, raw, 0.0).astype(BF16)


def selector(slot_ids, total):
    places = jnp.arange(total, dtype=jnp.int32)
    return (places[:, None] == slot_ids[None, :]).astype(BF16)


def pick_rows(select, flat):
    return lax.dot_general(
        select, flat, (((0,), (0,)), ((), ())), preferred_element_type=F32
    ).astype(BF16)


def place_rows(select, values):
    return jnp.dot(select, values, preferred_element_type=F32).astype(BF16)


def general_plan(queries, library, bucket, query_charge, library_charge):
    n_slab = lax.axis_size("slab")
    q_rows = queries.shape[0]
    width = queries.shape[1]
    cap = 2 * q_rows // n_slab
    query_unit = normalize(queries)
    library_unit = normalize(library)
    lib_charge = library_charge.astype(BF16)
    qcharge_col = query_charge.astype(BF16)[:, None]
    target = bucket[:, 0]
    positions = jnp.arange(q_rows, dtype=jnp.int32)
    earlier = (target[:, None] == target[None, :]) & (positions[None, :] < positions[:, None])
    rank = jnp.sum(earlier.astype(jnp.int32), axis=1)
    select_home = selector(target * cap + rank, n_slab * cap)
    outgoing = place_rows(select_home, query_unit).reshape(n_slab, cap, width)
    out_charge = place_rows(select_home, qcharge_col).reshape(n_slab, cap)
    below_rows, below_charge = passed_along((library_unit, lib_charge), "slab", 1)
    above_rows, above_charge = passed_along((library_unit, lib_charge), "slab", -1)
    rows = lax.all_to_all(outgoing, "slab", split_axis=0, concat_axis=0, tiled=True)
    charges = lax.all_to_all(out_charge, "slab", split_axis=0, concat_axis=0, tiled=True)
    count = rows.shape[1]
    flat = rows.reshape(n_slab * count, width)
    flat_charge = charges.reshape(n_slab * count)
    middle = score_block(flat, flat_charge, library_unit, lib_charge)
    lower = score_block(flat, flat_charge, below_rows, below_charge)
    upper = score_block(flat, flat_charge, above_rows, above_charge)
    joined = jnp.concatenate([lower, middle, upper], axis=1)
    joined = joined.reshape(n_slab, count, joined.shape[1])
    returned = lax.all_to_all(joined, "slab", split_axis=0, concat_axis=0, tiled=True)
    flat_back = returned.reshape(returned.shape[0] * returned.shape[1], returned.shape[2])
    return pick_rows(select_home, flat_back)


def swapped(value, mask):
    count = lax.axis_size("slab")
    return lax.ppermute(value, "slab", [(i, i ^ mask) for i in range(count)])


def unit_rows(values):
    values = values.astype(F32)
    return (values * lax.rsqrt(jnp.sum(values * values, axis=-1, keepdims=True) + EPS)).astype(BF16)


def slot_kernel(bucket_ref, qcharge_ref, lcharge_ref, slot_ref, qcharge_out, lcharge_out):
    q_rows = bucket_ref.shape[1]
    bucket = bucket_ref[...]
    along = jnp.broadcast_to(bucket.astype(F32), (q_rows, q_rows))
    i = lax.broadcasted_iota(jnp.int32, (q_rows, q_rows), 0)
    j = lax.broadcasted_iota(jnp.int32, (q_rows, q_rows), 1)
    earlier = jnp.where((along == along.T) & (i < j), 1.0, 0.0)
    rank = jnp.sum(earlier, axis=0, keepdims=True)
    slot_ref[...] = bucket * CAP + rank.astype(jnp.int32)
    for source, target in ((qcharge_ref, qcharge_out), (lcharge_ref, lcharge_out)):
        target[...] = jnp.broadcast_to(source[...].astype(F32), target.shape).astype(BF16)


def query_kernel(me_ref, slot_ref, charge_ref, q_ref, *out_refs):
    q_rows, width = q_ref.shape
    n_slots = (PLANE + 2) * CAP
    total = 4 * PLANE * CAP
    unit = unit_rows(q_ref[...])
    for k in range(4):
        plane = (me_ref[0] // PLANE) ^ k
        count = n_slots if k < 3 else n_slots - 2 * CAP
        skip = plane % 2 * (2 * CAP) if k == 3 else 0
        rel = (slot_ref[...] + (total - (plane * PLANE - 1) * CAP)) % total - skip
        place = lax.broadcasted_iota(jnp.int32, (q_rows, q_rows), 0) == rel
        select = jnp.where(place, 1.0, 0.0).astype(BF16)
        rows = jnp.dot(select[:count, :], unit, preferred_element_type=F32).astype(BF16)
        for n in range(width // 128):
            out_refs[k][n * count : (n + 1) * count, :] = rows[:, n * 128 : (n + 1) * 128]
        placed = lax.dot_general(
            charge_ref[...], select, (((1,), (1,)), ((), ())), preferred_element_type=F32
        )
        out_refs[k][width // 128 * count :, :] = placed.astype(BF16)


def unit_kernel(*refs):
    count = len(refs) // 2
    for source, target in zip(refs[:count], refs[count:]):
        for start in range(0, source.shape[0], 64):
            target[start : start + 64, :] = unit_rows(source[start : start + 64, :])


def pair_kernel(one_ref, other_ref, out_ref):
    line = lax.broadcasted_iota(jnp.int32, out_ref.shape, 0)
    one, other = one_ref[...].astype(F32), other_ref[...].astype(F32)
    out_ref[...] = jnp.where(line == 0, one, other).astype(BF16)


def score_kernel(count, turn, me_ref, *refs):
    q_refs, refs = refs[:count], refs[count:]
    lcharge_ref, lib_refs, out_refs = refs[0], refs[1:3], refs[3 : 3 + count]
    rows_ref, charge_ref = refs[3 + count :]
    n_slots, seen = (PLANE + 2) * CAP, 3 * CAP
    for n, lib in enumerate(lib_refs):
        width = lib.shape[1]
        at = pl.multiple_of(((me_ref[0] % PLANE) ^ (turn ^ n)) * CAP, CAP)
        for k in range(count):
            for c in range(width // 128):
                rows_ref[k * seen : (k + 1) * seen, c * 128 : (c + 1) * 128] = q_refs[k][
                    pl.ds(pl.multiple_of(at + c * n_slots, CAP), seen), :
                ]
            if n == 0:
                line = q_refs[k][width // 128 * n_slots :, :].astype(F32)[0:1, :]
                charge_ref[k] = jnp.broadcast_to(line, (128, 128)).T
        lib_charge = lcharge_ref[...].astype(F32)[n : n + 1, :]
        products = lax.dot_general(
            rows_ref[...], lib[...], (((1,), (1,)), ((), ())), preferred_element_type=F32
        )
        for k in range(count):
            row_charge = charge_ref[k, pl.ds(at, seen), :][:, 0:1]
            kept = jnp.abs(row_charge - lib_charge) <= 2.0
            out_refs[k][n * seen : (n + 1) * seen, :] = jnp.where(
                kept, products[k * seen : (k + 1) * seen, :], 0.0
            ).astype(BF16)


def first_kernel(me_ref, *refs):
    score_kernel(3, 0, me_ref, *refs[:9], *refs[10:])
    q_ref, out_ref = refs[0], refs[9]
    n_slots, shared = (PLANE + 2) * CAP, 2 * CAP
    count = (q_ref.shape[0] - META) // n_slots
    at = (1 - me_ref[0] // PLANE % 2) * (n_slots - shared)
    wide = out_ref.shape[1] // 128
    for n in range(count):
        row, column = n // wide * shared, n % wide * 128
        out_ref[row : row + shared, column : column + 128] = q_ref[
            pl.ds(pl.multiple_of(at + n * n_slots, CAP), shared), :
        ]
    row = count // wide * shared
    out_ref[row:, :] = jnp.zeros((META, out_ref.shape[1]), BF16)
    out_ref[row:, :128] = q_ref[count * n_slots :, :]


def second_kernel(me_ref, q_ref, passed_ref, *refs):
    charge_refs, lib_refs, out_ref, block_ref = refs[0], refs[1:3], refs[3], refs[4]
    rows_ref, charge_ref, column_ref = refs[5:]
    n_slots, shared = (PLANE + 2) * CAP, 2 * CAP
    part = n_slots - shared
    count = (q_ref.shape[0] - META) // part
    wide = passed_ref.shape[1] // 128
    odd = me_ref[0] // PLANE % 2
    own_at, passed_at = odd * shared, (1 - odd) * part
    for n in range(count):
        row, column = n // wide * shared, n % wide * 128
        block_ref[pl.ds(pl.multiple_of(n * n_slots + own_at, CAP), part), :] = q_ref[
            n * part : (n + 1) * part, :
        ]
        block_ref[pl.ds(pl.multiple_of(n * n_slots + passed_at, CAP), shared), :] = passed_ref[
            row : row + shared, column : column + 128
        ]
    row = count // wide * shared
    own_line = q_ref[count * part :, :].astype(F32)[0:1, :]
    passed_line = passed_ref[row:, :128].astype(F32)[0:1, :]
    column_ref[0] = jnp.broadcast_to(passed_line, (128, 128)).T
    column_ref[1] = jnp.broadcast_to(own_line, (128, 128)).T
    column_ref[2] = jnp.zeros((128, 128), F32)
    column_ref[2, pl.ds(pl.multiple_of(own_at, CAP), part), :] = column_ref[1, :part, :]
    column_ref[2, pl.ds(pl.multiple_of(passed_at, CAP), shared), :] = column_ref[
        0, pl.ds(pl.multiple_of(odd * part, CAP), shared), :
    ]
    block_ref[count * n_slots :, :] = column_ref[2].T[:META, :].astype(BF16)
    score_kernel(1, 0, me_ref, block_ref, charge_refs, *lib_refs, out_ref, rows_ref, charge_ref)


def home_kernel(me_ref, slot_ref, *refs):
    near8, near12, near4, near0, far8, far4, far12, far0, out_ref, flat_ref = refs
    near = [near0, near4, near8, near12]
    far = [far0, far4, far8, far12]
    q_rows = slot_ref.shape[1]
    l_rows = near0.shape[1]
    n_slab = 4 * PLANE
    total = n_slab * CAP
    slot = slot_ref[...]
    bucket, rank = slot // CAP, slot % CAP
    places = lax.broadcasted_iota(jnp.int32, (total, q_rows), 0)
    for unit in range(3):
        for m in range(n_slab):
            ref = (far if m & 2 else near)[m // PLANE]
            at = (m & 1) * 3 * CAP + (2 - unit) * CAP
            flat_ref[m * CAP : (m + 1) * CAP, :] = ref[at : at + CAP, :]
        slab = (bucket + (unit - 1 + n_slab)) % n_slab
        want = (slab ^ me_ref[0]) * CAP + rank
        select = jnp.where(places == want, 1.0, 0.0).T.astype(BF16)
        out_ref[:, unit * l_rows : (unit + 1) * l_rows] = jnp.dot(
            select, flat_ref[...], preferred_element_type=F32
        ).astype(BF16)


VMEM = pl.BlockSpec(memory_space=pltpu.VMEM)
SMEM = pl.BlockSpec(memory_space=pltpu.SMEM)


MIB = 1024 * 1024


def kernel_call(body, outs, args, specs, scratch=(), cost=1):
    return pl.pallas_call(
        body,
        out_shape=[jax.ShapeDtypeStruct(o.shape, o.dtype) for o in outs],
        in_specs=specs,
        out_specs=[VMEM] * len(outs),
        scratch_shapes=scratch,
        compiler_params=pltpu.CompilerParams(vmem_limit_bytes=12 * MIB),
        cost_estimate=pl.CostEstimate(flops=0, bytes_accessed=cost, transcendentals=0),
    )(*args)


def shape(*dims, dtype=BF16):
    return jax.ShapeDtypeStruct(dims, dtype)


def line_plan(queries, library, bucket, query_charge, library_charge):
    q_rows, width = queries.shape
    l_rows = library.shape[0]
    me = lax.axis_index("slab").astype(jnp.int32).reshape(1)
    n_slots, seen = (PLANE + 2) * CAP, 3 * CAP
    int32 = jnp.int32
    raw_y, raw_c = swapped(library, 2), swapped(library, 1)
    slot, qcharge, charge = kernel_call(
        slot_kernel,
        [shape(1, q_rows, dtype=int32), shape(META, q_rows), shape(META, l_rows)],
        [x.reshape(1, -1) for x in (bucket, query_charge, library_charge)],
        [VMEM] * 3,
        cost=1,
    )
    slots_shape = shape(width // 128 * n_slots + META, 128)
    q0, q4, q8, q12 = kernel_call(
        query_kernel,
        [slots_shape] * 3 + [shape(width // 128 * (n_slots - 2 * CAP) + META, 128)],
        [me, slot, qcharge, queries],
        [SMEM] + [VMEM] * 3,
    )
    q12, q8, q4 = swapped(q12, 12), swapped(q8, 8), swapped(q4, 4)
    lib = shape(l_rows, width)
    unit, unit_c = kernel_call(unit_kernel, [lib] * 2, [library, raw_c], [VMEM] * 2)
    charge_c = swapped(charge, 1)
    (near_charge,) = kernel_call(pair_kernel, [charge], [charge, charge_c], [VMEM] * 2)
    far_charge = swapped(near_charge, 2)

    block = shape(2 * seen, l_rows)
    shared_rows = width // l_rows * 2 * CAP + META
    first = [q8, q4, q0, near_charge, unit, unit_c]
    near8, near4, near0, passed = kernel_call(
        first_kernel,
        [block] * 3 + [shape(shared_rows, l_rows)],
        [me, *first],
        [SMEM] + [VMEM] * len(first),
        [pltpu.VMEM((3 * seen, width), BF16), pltpu.VMEM((3, 128, 128), F32)],
    )
    near8, passed = swapped(near8, 8), swapped(passed, 4)
    near12, q12 = kernel_call(
        second_kernel,
        [block, slots_shape],
        [me, q12, passed, near_charge, unit, unit_c],
        [SMEM] + [VMEM] * 5,
        [
            pltpu.VMEM((seen, width), BF16),
            pltpu.VMEM((1, 128, 128), F32),
            pltpu.VMEM((3, 128, 128), F32),
        ],
    )
    raw_y, near8, near4, near12, far_charge = lax.optimization_barrier(
        (raw_y, near8, near4, near12, far_charge)
    )
    raw_d = swapped(raw_y, 1)
    near12, near4 = swapped(near12, 12), swapped(near4, 4)
    (unit_y,) = kernel_call(unit_kernel, [lib], [raw_y], [VMEM])
    (unit_d,) = kernel_call(unit_kernel, [lib], [raw_d], [VMEM])
    far8, far4, far12, far0 = kernel_call(
        functools.partial(score_kernel, 4, 2),
        [block] * 4,
        [me, q8, q4, q12, q0, far_charge, unit_y, unit_d],
        [SMEM] + [VMEM] * 7,
        [pltpu.VMEM((4 * seen, width), BF16), pltpu.VMEM((4, 128, 128), F32)],
    )
    far8, far4, far12 = swapped(far8, 8), swapped(far4, 4), swapped(far12, 12)
    (out,) = kernel_call(
        home_kernel,
        [shape(q_rows, 3 * l_rows)],
        [me, slot, near8, near12, near4, near0, far8, far4, far12, far0],
        [SMEM] + [VMEM] * 9,
        [pltpu.VMEM((4 * PLANE * CAP, l_rows), BF16)],
    )
    return out


def per_device(queries, library, bucket, query_charge, library_charge):
    n_slab = lax.axis_size("slab")
    q_rows, width = queries.shape
    fits = n_slab == 4 * PLANE and 2 * q_rows == n_slab * CAP and q_rows == 128
    plan = line_plan if fits and width % 256 == 0 and width % (2 * library.shape[0]) == 0 else general_plan
    return plan(queries, library, bucket, query_charge, library_charge)


def solution(mesh):
    placed = (
        P(("grp", "slab"), None),
        P(("grp", "slab"), None),
        P(("grp", "slab"), None),
        P(("grp", "slab")),
        P(("grp", "slab")),
    )
    return jax.shard_map(
        per_device, mesh=mesh, in_specs=placed, out_specs=P(("grp", "slab"), None), check_vma=False
    )
```

```python
import functools

import jax
import jax.numpy as jnp
from jax import lax
from jax.experimental import pallas as pl
from jax.experimental.pallas import tpu as pltpu
from jax.sharding import PartitionSpec as P

EPS = 1e-06
PLANE = 4
CAP = 16
META = 16
F32 = jnp.float32
BF16 = jnp.bfloat16


def passed_along(value, axis, steps):
    count = lax.axis_size(axis)
    pairs = [(source, (source + steps) % count) for source in range(count)]
    return lax.ppermute(value, axis, pairs)


def normalize(rows):
    values = rows.astype(F32)
    return (values * lax.rsqrt(jnp.sum(values * values, axis=-1, keepdims=True) + EPS)).astype(BF16)


def score_block(rows, row_charge, lib_rows, lib_charge):
    raw = lax.dot_general(rows, lib_rows, (((1,), (1,)), ((), ())), preferred_element_type=F32)
    keep = jnp.abs(row_charge.astype(F32)[:, None] - lib_charge.astype(F32)[None, :]) <= 2.0
    return jnp.where(keep, raw, 0.0).astype(BF16)


def selector(slot_ids, total):
    places = jnp.arange(total, dtype=jnp.int32)
    return (places[:, None] == slot_ids[None, :]).astype(BF16)


def pick_rows(select, flat):
    return lax.dot_general(
        select, flat, (((0,), (0,)), ((), ())), preferred_element_type=F32
    ).astype(BF16)


def place_rows(select, values):
    return jnp.dot(select, values, preferred_element_type=F32).astype(BF16)


def general_plan(queries, library, bucket, query_charge, library_charge):
    n_slab = lax.axis_size("slab")
    q_rows = queries.shape[0]
    width = queries.shape[1]
    cap = 2 * q_rows // n_slab
    query_unit = normalize(queries)
    library_unit = normalize(library)
    lib_charge = library_charge.astype(BF16)
    qcharge_col = query_charge.astype(BF16)[:, None]
    target = bucket[:, 0]
    positions = jnp.arange(q_rows, dtype=jnp.int32)
    earlier = (target[:, None] == target[None, :]) & (positions[None, :] < positions[:, None])
    rank = jnp.sum(earlier.astype(jnp.int32), axis=1)
    select_home = selector(target * cap + rank, n_slab * cap)
    outgoing = place_rows(select_home, query_unit).reshape(n_slab, cap, width)
    out_charge = place_rows(select_home, qcharge_col).reshape(n_slab, cap)
    below_rows, below_charge = passed_along((library_unit, lib_charge), "slab", 1)
    above_rows, above_charge = passed_along((library_unit, lib_charge), "slab", -1)
    rows = lax.all_to_all(outgoing, "slab", split_axis=0, concat_axis=0, tiled=True)
    charges = lax.all_to_all(out_charge, "slab", split_axis=0, concat_axis=0, tiled=True)
    count = rows.shape[1]
    flat = rows.reshape(n_slab * count, width)
    flat_charge = charges.reshape(n_slab * count)
    middle = score_block(flat, flat_charge, library_unit, lib_charge)
    lower = score_block(flat, flat_charge, below_rows, below_charge)
    upper = score_block(flat, flat_charge, above_rows, above_charge)
    joined = jnp.concatenate([lower, middle, upper], axis=1)
    joined = joined.reshape(n_slab, count, joined.shape[1])
    returned = lax.all_to_all(joined, "slab", split_axis=0, concat_axis=0, tiled=True)
    flat_back = returned.reshape(returned.shape[0] * returned.shape[1], returned.shape[2])
    return pick_rows(select_home, flat_back)


def swapped(value, mask):
    count = lax.axis_size("slab")
    return lax.ppermute(value, "slab", [(i, i ^ mask) for i in range(count)])


def unit_rows(values):
    values = values.astype(F32)
    return (values * lax.rsqrt(jnp.sum(values * values, axis=-1, keepdims=True) + EPS)).astype(BF16)


def slot_kernel(bucket_ref, qcharge_ref, lcharge_ref, slot_ref, qcharge_out, lcharge_out):
    q_rows = bucket_ref.shape[1]
    bucket = bucket_ref[...]
    along = jnp.broadcast_to(bucket.astype(F32), (q_rows, q_rows))
    i = lax.broadcasted_iota(jnp.int32, (q_rows, q_rows), 0)
    j = lax.broadcasted_iota(jnp.int32, (q_rows, q_rows), 1)
    earlier = jnp.where((along == along.T) & (i < j), 1.0, 0.0)
    rank = jnp.sum(earlier, axis=0, keepdims=True)
    slot_ref[...] = bucket * CAP + rank.astype(jnp.int32)
    for source, target in ((qcharge_ref, qcharge_out), (lcharge_ref, lcharge_out)):
        target[...] = jnp.broadcast_to(source[...].astype(F32), target.shape).astype(BF16)


def query_kernel(me_ref, slot_ref, charge_ref, q_ref, *out_refs):
    q_rows, width = q_ref.shape
    n_slots = (PLANE + 2) * CAP
    total = 4 * PLANE * CAP
    unit = unit_rows(q_ref[...])
    for k in range(4):
        plane = (me_ref[0] // PLANE) ^ k
        count = n_slots if k < 3 else n_slots - 2 * CAP
        skip = plane % 2 * (2 * CAP) if k == 3 else 0
        rel = (slot_ref[...] + (total - (plane * PLANE - 1) * CAP)) % total - skip
        place = lax.broadcasted_iota(jnp.int32, (q_rows, q_rows), 0) == rel
        select = jnp.where(place, 1.0, 0.0).astype(BF16)
        rows = jnp.dot(select[:count, :], unit, preferred_element_type=F32).astype(BF16)
        for n in range(width // 128):
            out_refs[k][n * count : (n + 1) * count, :] = rows[:, n * 128 : (n + 1) * 128]
        placed = lax.dot_general(
            charge_ref[...], select, (((1,), (1,)), ((), ())), preferred_element_type=F32
        )
        out_refs[k][width // 128 * count :, :] = placed.astype(BF16)


def unit_kernel(*refs):
    count = len(refs) // 2
    for source, target in zip(refs[:count], refs[count:]):
        for start in range(0, source.shape[0], 64):
            target[start : start + 64, :] = unit_rows(source[start : start + 64, :])


def pair_kernel(one_ref, other_ref, out_ref):
    line = lax.broadcasted_iota(jnp.int32, out_ref.shape, 0)
    one, other = one_ref[...].astype(F32), other_ref[...].astype(F32)
    out_ref[...] = jnp.where(line == 0, one, other).astype(BF16)


def score_kernel(count, turn, me_ref, *refs):
    q_refs, refs = refs[:count], refs[count:]
    lcharge_ref, lib_refs, out_refs = refs[0], refs[1:3], refs[3 : 3 + count]
    rows_ref, charge_ref = refs[3 + count :]
    n_slots, seen = (PLANE + 2) * CAP, 3 * CAP
    for n, lib in enumerate(lib_refs):
        width = lib.shape[1]
        at = pl.multiple_of(((me_ref[0] % PLANE) ^ (turn ^ n)) * CAP, CAP)
        for k in range(count):
            for c in range(width // 128):
                rows_ref[k * seen : (k + 1) * seen, c * 128 : (c + 1) * 128] = q_refs[k][
                    pl.ds(pl.multiple_of(at + c * n_slots, CAP), seen), :
                ]
            if n == 0:
                line = q_refs[k][width // 128 * n_slots :, :].astype(F32)[0:1, :]
                charge_ref[k] = jnp.broadcast_to(line, (128, 128)).T
        lib_charge = lcharge_ref[...].astype(F32)[n : n + 1, :]
        products = lax.dot_general(
            rows_ref[...], lib[...], (((1,), (1,)), ((), ())), preferred_element_type=F32
        )
        for k in range(count):
            row_charge = charge_ref[k, pl.ds(at, seen), :][:, 0:1]
            kept = jnp.abs(row_charge - lib_charge) <= 2.0
            out_refs[k][n * seen : (n + 1) * seen, :] = jnp.where(
                kept, products[k * seen : (k + 1) * seen, :], 0.0
            ).astype(BF16)


def first_kernel(me_ref, *refs):
    score_kernel(3, 0, me_ref, *refs[:9], *refs[10:])
    q_ref, out_ref = refs[0], refs[9]
    n_slots, shared = (PLANE + 2) * CAP, 2 * CAP
    count = (q_ref.shape[0] - META) // n_slots
    at = (1 - me_ref[0] // PLANE % 2) * (n_slots - shared)
    wide = out_ref.shape[1] // 128
    for n in range(count):
        row, column = n // wide * shared, n % wide * 128
        out_ref[row : row + shared, column : column + 128] = q_ref[
            pl.ds(pl.multiple_of(at + n * n_slots, CAP), shared), :
        ]
    row = count // wide * shared
    out_ref[row:, :] = jnp.zeros((META, out_ref.shape[1]), BF16)
    out_ref[row:, :128] = q_ref[count * n_slots :, :]


def second_kernel(me_ref, q_ref, passed_ref, *refs):
    charge_refs, lib_refs, out_ref, block_ref = refs[0], refs[1:3], refs[3], refs[4]
    rows_ref, charge_ref, column_ref = refs[5:]
    n_slots, shared = (PLANE + 2) * CAP, 2 * CAP
    part = n_slots - shared
    count = (q_ref.shape[0] - META) // part
    wide = passed_ref.shape[1] // 128
    odd = me_ref[0] // PLANE % 2
    own_at, passed_at = odd * shared, (1 - odd) * part
    for n in range(count):
        row, column = n // wide * shared, n % wide * 128
        block_ref[pl.ds(pl.multiple_of(n * n_slots + own_at, CAP), part), :] = q_ref[
            n * part : (n + 1) * part, :
        ]
        block_ref[pl.ds(pl.multiple_of(n * n_slots + passed_at, CAP), shared), :] = passed_ref[
            row : row + shared, column : column + 128
        ]
    row = count // wide * shared
    own_line = q_ref[count * part :, :].astype(F32)[0:1, :]
    passed_line = passed_ref[row:, :128].astype(F32)[0:1, :]
    column_ref[0] = jnp.broadcast_to(passed_line, (128, 128)).T
    column_ref[1] = jnp.broadcast_to(own_line, (128, 128)).T
    column_ref[2] = jnp.zeros((128, 128), F32)
    column_ref[2, pl.ds(pl.multiple_of(own_at, CAP), part), :] = column_ref[1, :part, :]
    column_ref[2, pl.ds(pl.multiple_of(passed_at, CAP), shared), :] = column_ref[
        0, pl.ds(pl.multiple_of(odd * part, CAP), shared), :
    ]
    block_ref[count * n_slots :, :] = column_ref[2].T[:META, :].astype(BF16)
    score_kernel(1, 0, me_ref, block_ref, charge_refs, *lib_refs, out_ref, rows_ref, charge_ref)


def far_kernel(part, me_ref, *refs):
    q_refs, lcharge_ref, raw_ref, refs = refs[:4], refs[4], refs[5], refs[6:]
    upper_refs, refs = (refs[:4], refs[4:]) if part else ((), refs)
    out_refs, (rows_ref, charge_ref, unit_ref) = refs[:4], refs[4:]
    n_slots, seen = (PLANE + 2) * CAP, 3 * CAP
    for start in range(0, raw_ref.shape[0], 64):
        unit_ref[start : start + 64, :] = unit_rows(raw_ref[start : start + 64, :])
    at = pl.multiple_of(((me_ref[0] % PLANE) ^ (2 + part)) * CAP, CAP)
    chunks = raw_ref.shape[1] // 128
    for k in range(4):
        for c in range(chunks):
            rows_ref[k * seen : (k + 1) * seen, c * 128 : (c + 1) * 128] = q_refs[k][
                pl.ds(pl.multiple_of(at + c * n_slots, CAP), seen), :
            ]
        line = q_refs[k][chunks * n_slots :, :].astype(F32)[0:1, :]
        charge_ref[k] = jnp.broadcast_to(line, (128, 128)).T
    lib_charge = lcharge_ref[...].astype(F32)[part : part + 1, :]
    products = lax.dot_general(
        rows_ref[...], unit_ref[...], (((1,), (1,)), ((), ())), preferred_element_type=F32
    )
    for k in range(4):
        row_charge = charge_ref[k, pl.ds(at, seen), :][:, 0:1]
        kept = jnp.abs(row_charge - lib_charge) <= 2.0
        scores = jnp.where(kept, products[k * seen : (k + 1) * seen, :], 0.0).astype(BF16)
        if part:
            out_refs[k][:seen, :] = upper_refs[k][...]
        out_refs[k][part * seen : (part + 1) * seen, :] = scores


def home_kernel(me_ref, slot_ref, *refs):
    near8, near12, near4, near0, far8, far4, far12, far0, out_ref, flat_ref = refs
    near = [near0, near4, near8, near12]
    far = [far0, far4, far8, far12]
    q_rows = slot_ref.shape[1]
    l_rows = near0.shape[1]
    n_slab = 4 * PLANE
    total = n_slab * CAP
    slot = slot_ref[...]
    bucket, rank = slot // CAP, slot % CAP
    places = lax.broadcasted_iota(jnp.int32, (total, q_rows), 0)
    for unit in range(3):
        for m in range(n_slab):
            ref = (far if m & 2 else near)[m // PLANE]
            at = (m & 1) * 3 * CAP + (2 - unit) * CAP
            flat_ref[m * CAP : (m + 1) * CAP, :] = ref[at : at + CAP, :]
        slab = (bucket + (unit - 1 + n_slab)) % n_slab
        want = (slab ^ me_ref[0]) * CAP + rank
        select = jnp.where(places == want, 1.0, 0.0).T.astype(BF16)
        out_ref[:, unit * l_rows : (unit + 1) * l_rows] = jnp.dot(
            select, flat_ref[...], preferred_element_type=F32
        ).astype(BF16)


VMEM = pl.BlockSpec(memory_space=pltpu.VMEM)
SMEM = pl.BlockSpec(memory_space=pltpu.SMEM)


MIB = 1024 * 1024


def kernel_call(body, outs, args, specs, scratch=(), cost=1):
    return pl.pallas_call(
        body,
        out_shape=[jax.ShapeDtypeStruct(o.shape, o.dtype) for o in outs],
        in_specs=specs,
        out_specs=[VMEM] * len(outs),
        scratch_shapes=scratch,
        compiler_params=pltpu.CompilerParams(vmem_limit_bytes=12 * MIB),
        cost_estimate=pl.CostEstimate(flops=0, bytes_accessed=cost, transcendentals=0),
    )(*args)


def shape(*dims, dtype=BF16):
    return jax.ShapeDtypeStruct(dims, dtype)


def line_plan(queries, library, bucket, query_charge, library_charge):
    q_rows, width = queries.shape
    l_rows = library.shape[0]
    me = lax.axis_index("slab").astype(jnp.int32).reshape(1)
    n_slots, seen = (PLANE + 2) * CAP, 3 * CAP
    int32 = jnp.int32
    raw_y, raw_c = swapped(library, 2), swapped(library, 1)
    slot, qcharge, charge = kernel_call(
        slot_kernel,
        [shape(1, q_rows, dtype=int32), shape(META, q_rows), shape(META, l_rows)],
        [x.reshape(1, -1) for x in (bucket, query_charge, library_charge)],
        [VMEM] * 3,
        cost=1,
    )
    slots_shape = shape(width // 128 * n_slots + META, 128)
    q0, q4, q8, q12 = kernel_call(
        query_kernel,
        [slots_shape] * 3 + [shape(width // 128 * (n_slots - 2 * CAP) + META, 128)],
        [me, slot, qcharge, queries],
        [SMEM] + [VMEM] * 3,
    )
    q12, q8, q4 = swapped(q12, 12), swapped(q8, 8), swapped(q4, 4)
    lib = shape(l_rows, width)
    unit, unit_c = kernel_call(unit_kernel, [lib] * 2, [library, raw_c], [VMEM] * 2)
    charge_c = swapped(charge, 1)
    (near_charge,) = kernel_call(pair_kernel, [charge], [charge, charge_c], [VMEM] * 2)
    far_charge = swapped(near_charge, 2)

    block = shape(2 * seen, l_rows)
    shared_rows = width // l_rows * 2 * CAP + META
    first = [q8, q4, q0, near_charge, unit, unit_c]
    near8, near4, near0, passed = kernel_call(
        first_kernel,
        [block] * 3 + [shape(shared_rows, l_rows)],
        [me, *first],
        [SMEM] + [VMEM] * len(first),
        [pltpu.VMEM((3 * seen, width), BF16), pltpu.VMEM((3, 128, 128), F32)],
    )
    near8, passed = swapped(near8, 8), swapped(passed, 4)
    near12, q12 = kernel_call(
        second_kernel,
        [block, slots_shape],
        [me, q12, passed, near_charge, unit, unit_c],
        [SMEM] + [VMEM] * 5,
        [
            pltpu.VMEM((seen, width), BF16),
            pltpu.VMEM((1, 128, 128), F32),
            pltpu.VMEM((3, 128, 128), F32),
        ],
    )
    raw_y, near8, near4, near12, far_charge = lax.optimization_barrier(
        (raw_y, near8, near4, near12, far_charge)
    )
    raw_d = swapped(raw_y, 1)
    near12, near4 = swapped(near12, 12), swapped(near4, 4)
    upper = ()
    for part, raw in enumerate((raw_y, raw_d)):
        upper = kernel_call(
            functools.partial(far_kernel, part),
            [shape((part + 1) * seen, l_rows)] * 4,
            [me, q8, q4, q12, q0, far_charge, raw, *upper],
            [SMEM] + [VMEM] * (6 + len(upper)),
            [
                pltpu.VMEM((4 * seen, width), BF16),
                pltpu.VMEM((4, 128, 128), F32),
                pltpu.VMEM((l_rows, width), BF16),
            ],
        )
    far8, far4, far12, far0 = upper
    far8, far4, far12 = swapped(far8, 8), swapped(far4, 4), swapped(far12, 12)
    (out,) = kernel_call(
        home_kernel,
        [shape(q_rows, 3 * l_rows)],
        [me, slot, near8, near12, near4, near0, far8, far4, far12, far0],
        [SMEM] + [VMEM] * 9,
        [pltpu.VMEM((4 * PLANE * CAP, l_rows), BF16)],
    )
    return out


def per_device(queries, library, bucket, query_charge, library_charge):
    n_slab = lax.axis_size("slab")
    q_rows, width = queries.shape
    fits = n_slab == 4 * PLANE and 2 * q_rows == n_slab * CAP and q_rows == 128
    plan = line_plan if fits and width % 256 == 0 and width % (2 * library.shape[0]) == 0 else general_plan
    return plan(queries, library, bucket, query_charge, library_charge)


def solution(mesh):
    placed = (
        P(("grp", "slab"), None),
        P(("grp", "slab"), None),
        P(("grp", "slab"), None),
        P(("grp", "slab")),
        P(("grp", "slab")),
    )
    return jax.shard_map(
        per_device, mesh=mesh, in_specs=placed, out_specs=P(("grp", "slab"), None), check_vma=False
    )
```

```python
import functools

import jax
import jax.numpy as jnp
from jax import lax
from jax.experimental import pallas as pl
from jax.experimental.pallas import tpu as pltpu
from jax.sharding import PartitionSpec as P

EPS = 1e-06
PLANE = 4
CAP = 16
META = 16
F32 = jnp.float32
BF16 = jnp.bfloat16


def passed_along(value, axis, steps):
    count = lax.axis_size(axis)
    pairs = [(source, (source + steps) % count) for source in range(count)]
    return lax.ppermute(value, axis, pairs)


def normalize(rows):
    values = rows.astype(F32)
    return (values * lax.rsqrt(jnp.sum(values * values, axis=-1, keepdims=True) + EPS)).astype(BF16)


def score_block(rows, row_charge, lib_rows, lib_charge):
    raw = lax.dot_general(rows, lib_rows, (((1,), (1,)), ((), ())), preferred_element_type=F32)
    keep = jnp.abs(row_charge.astype(F32)[:, None] - lib_charge.astype(F32)[None, :]) <= 2.0
    return jnp.where(keep, raw, 0.0).astype(BF16)


def selector(slot_ids, total):
    places = jnp.arange(total, dtype=jnp.int32)
    return (places[:, None] == slot_ids[None, :]).astype(BF16)


def pick_rows(select, flat):
    return lax.dot_general(
        select, flat, (((0,), (0,)), ((), ())), preferred_element_type=F32
    ).astype(BF16)


def place_rows(select, values):
    return jnp.dot(select, values, preferred_element_type=F32).astype(BF16)


def general_plan(queries, library, bucket, query_charge, library_charge):
    n_slab = lax.axis_size("slab")
    q_rows = queries.shape[0]
    width = queries.shape[1]
    cap = 2 * q_rows // n_slab
    query_unit = normalize(queries)
    library_unit = normalize(library)
    lib_charge = library_charge.astype(BF16)
    qcharge_col = query_charge.astype(BF16)[:, None]
    target = bucket[:, 0]
    positions = jnp.arange(q_rows, dtype=jnp.int32)
    earlier = (target[:, None] == target[None, :]) & (positions[None, :] < positions[:, None])
    rank = jnp.sum(earlier.astype(jnp.int32), axis=1)
    select_home = selector(target * cap + rank, n_slab * cap)
    outgoing = place_rows(select_home, query_unit).reshape(n_slab, cap, width)
    out_charge = place_rows(select_home, qcharge_col).reshape(n_slab, cap)
    below_rows, below_charge = passed_along((library_unit, lib_charge), "slab", 1)
    above_rows, above_charge = passed_along((library_unit, lib_charge), "slab", -1)
    rows = lax.all_to_all(outgoing, "slab", split_axis=0, concat_axis=0, tiled=True)
    charges = lax.all_to_all(out_charge, "slab", split_axis=0, concat_axis=0, tiled=True)
    count = rows.shape[1]
    flat = rows.reshape(n_slab * count, width)
    flat_charge = charges.reshape(n_slab * count)
    middle = score_block(flat, flat_charge, library_unit, lib_charge)
    lower = score_block(flat, flat_charge, below_rows, below_charge)
    upper = score_block(flat, flat_charge, above_rows, above_charge)
    joined = jnp.concatenate([lower, middle, upper], axis=1)
    joined = joined.reshape(n_slab, count, joined.shape[1])
    returned = lax.all_to_all(joined, "slab", split_axis=0, concat_axis=0, tiled=True)
    flat_back = returned.reshape(returned.shape[0] * returned.shape[1], returned.shape[2])
    return pick_rows(select_home, flat_back)


def swapped(value, mask):
    count = lax.axis_size("slab")
    return lax.ppermute(value, "slab", [(i, i ^ mask) for i in range(count)])


def unit_rows(values):
    values = values.astype(F32)
    return (values * lax.rsqrt(jnp.sum(values * values, axis=-1, keepdims=True) + EPS)).astype(BF16)


def slot_kernel(bucket_ref, qcharge_ref, lcharge_ref, slot_ref, qcharge_out, lcharge_out):
    q_rows = bucket_ref.shape[1]
    bucket = bucket_ref[...]
    along = jnp.broadcast_to(bucket.astype(F32), (q_rows, q_rows))
    i = lax.broadcasted_iota(jnp.int32, (q_rows, q_rows), 0)
    j = lax.broadcasted_iota(jnp.int32, (q_rows, q_rows), 1)
    earlier = jnp.where((along == along.T) & (i < j), 1.0, 0.0)
    rank = jnp.sum(earlier, axis=0, keepdims=True)
    slot_ref[...] = bucket * CAP + rank.astype(jnp.int32)
    for source, target in ((qcharge_ref, qcharge_out), (lcharge_ref, lcharge_out)):
        target[...] = jnp.broadcast_to(source[...].astype(F32), target.shape).astype(BF16)


def query_kernel(me_ref, slot_ref, charge_ref, q_ref, *out_refs):
    q_rows, width = q_ref.shape
    n_slots = (PLANE + 2) * CAP
    total = 4 * PLANE * CAP
    unit = unit_rows(q_ref[...])
    for k in range(4):
        plane = (me_ref[0] // PLANE) ^ k
        count = n_slots if k < 3 else n_slots - 2 * CAP
        skip = plane % 2 * (2 * CAP) if k == 3 else 0
        rel = (slot_ref[...] + (total - (plane * PLANE - 1) * CAP)) % total - skip
        place = lax.broadcasted_iota(jnp.int32, (q_rows, q_rows), 0) == rel
        select = jnp.where(place, 1.0, 0.0).astype(BF16)
        rows = jnp.dot(select[:count, :], unit, preferred_element_type=F32).astype(BF16)
        for n in range(width // 128):
            out_refs[k][n * count : (n + 1) * count, :] = rows[:, n * 128 : (n + 1) * 128]
        placed = lax.dot_general(
            charge_ref[...], select, (((1,), (1,)), ((), ())), preferred_element_type=F32
        )
        out_refs[k][width // 128 * count :, :] = placed.astype(BF16)


def unit_kernel(*refs):
    count = len(refs) // 2
    for source, target in zip(refs[:count], refs[count:]):
        for start in range(0, source.shape[0], 64):
            target[start : start + 64, :] = unit_rows(source[start : start + 64, :])


def pair_kernel(one_ref, other_ref, out_ref):
    line = lax.broadcasted_iota(jnp.int32, out_ref.shape, 0)
    one, other = one_ref[...].astype(F32), other_ref[...].astype(F32)
    out_ref[...] = jnp.where(line == 0, one, other).astype(BF16)


def score_kernel(count, turn, me_ref, *refs):
    q_refs, refs = refs[:count], refs[count:]
    lcharge_ref, lib_refs, out_refs = refs[0], refs[1:3], refs[3 : 3 + count]
    rows_ref, charge_ref = refs[3 + count :]
    n_slots, seen = (PLANE + 2) * CAP, 3 * CAP
    for n, lib in enumerate(lib_refs):
        width = lib.shape[1]
        at = pl.multiple_of(((me_ref[0] % PLANE) ^ (turn ^ n)) * CAP, CAP)
        for k in range(count):
            for c in range(width // 128):
                rows_ref[k * seen : (k + 1) * seen, c * 128 : (c + 1) * 128] = q_refs[k][
                    pl.ds(pl.multiple_of(at + c * n_slots, CAP), seen), :
                ]
            if n == 0:
                line = q_refs[k][width // 128 * n_slots :, :].astype(F32)[0:1, :]
                charge_ref[k] = jnp.broadcast_to(line, (128, 128)).T
        lib_charge = lcharge_ref[...].astype(F32)[n : n + 1, :]
        products = lax.dot_general(
            rows_ref[...], lib[...], (((1,), (1,)), ((), ())), preferred_element_type=F32
        )
        for k in range(count):
            row_charge = charge_ref[k, pl.ds(at, seen), :][:, 0:1]
            kept = jnp.abs(row_charge - lib_charge) <= 2.0
            out_refs[k][n * seen : (n + 1) * seen, :] = jnp.where(
                kept, products[k * seen : (k + 1) * seen, :], 0.0
            ).astype(BF16)


def first_kernel(me_ref, *refs):
    score_kernel(3, 0, me_ref, *refs[:9], *refs[10:])
    q_ref, out_ref = refs[0], refs[9]
    n_slots, shared = (PLANE + 2) * CAP, 2 * CAP
    count = (q_ref.shape[0] - META) // n_slots
    at = (1 - me_ref[0] // PLANE % 2) * (n_slots - shared)
    wide = out_ref.shape[1] // 128
    for n in range(count):
        row, column = n // wide * shared, n % wide * 128
        out_ref[row : row + shared, column : column + 128] = q_ref[
            pl.ds(pl.multiple_of(at + n * n_slots, CAP), shared), :
        ]
    row = count // wide * shared
    out_ref[row:, :] = jnp.zeros((out_ref.shape[0] - row, out_ref.shape[1]), BF16)
    out_ref[row : row + META, :128] = q_ref[count * n_slots :, :]


def second_kernel(me_ref, q_ref, passed_ref, *refs):
    charge_refs, lib_refs, out_ref, block_ref = refs[0], refs[1:3], refs[3], refs[4]
    rows_ref, charge_ref, column_ref = refs[5:]
    n_slots, shared = (PLANE + 2) * CAP, 2 * CAP
    part = n_slots - shared
    count = (q_ref.shape[0] - META) // part
    wide = passed_ref.shape[1] // 128
    odd = me_ref[0] // PLANE % 2
    own_at, passed_at = odd * shared, (1 - odd) * part
    for n in range(count):
        row, column = n // wide * shared, n % wide * 128
        block_ref[pl.ds(pl.multiple_of(n * n_slots + own_at, CAP), part), :] = q_ref[
            n * part : (n + 1) * part, :
        ]
        block_ref[pl.ds(pl.multiple_of(n * n_slots + passed_at, CAP), shared), :] = passed_ref[
            row : row + shared, column : column + 128
        ]
    row = count // wide * shared
    own_line = q_ref[count * part :, :].astype(F32)[0:1, :]
    passed_line = passed_ref[row:, :128].astype(F32)[0:1, :]
    column_ref[0] = jnp.broadcast_to(passed_line, (128, 128)).T
    column_ref[1] = jnp.broadcast_to(own_line, (128, 128)).T
    column_ref[2] = jnp.zeros((128, 128), F32)
    column_ref[2, pl.ds(pl.multiple_of(own_at, CAP), part), :] = column_ref[1, :part, :]
    column_ref[2, pl.ds(pl.multiple_of(passed_at, CAP), shared), :] = column_ref[
        0, pl.ds(pl.multiple_of(odd * part, CAP), shared), :
    ]
    block_ref[count * n_slots :, :] = column_ref[2].T[:META, :].astype(BF16)
    score_kernel(1, 0, me_ref, block_ref, charge_refs, *lib_refs, out_ref, rows_ref, charge_ref)


def far_kernel(part, me_ref, *refs):
    q_refs, lcharge_ref, raw_ref, refs = refs[:4], refs[4], refs[5], refs[6:]
    upper_refs, refs = (refs[:4], refs[4:]) if part else ((), refs)
    out_refs, (rows_ref, charge_ref, unit_ref) = refs[:4], refs[4:]
    n_slots, seen = (PLANE + 2) * CAP, 3 * CAP
    for start in range(0, raw_ref.shape[0], 64):
        unit_ref[start : start + 64, :] = unit_rows(raw_ref[start : start + 64, :])
    at = pl.multiple_of(((me_ref[0] % PLANE) ^ (2 + part)) * CAP, CAP)
    chunks = raw_ref.shape[1] // 128
    for k in range(4):
        for c in range(chunks):
            rows_ref[k * seen : (k + 1) * seen, c * 128 : (c + 1) * 128] = q_refs[k][
                pl.ds(pl.multiple_of(at + c * n_slots, CAP), seen), :
            ]
        line = q_refs[k][chunks * n_slots :, :].astype(F32)[0:1, :]
        charge_ref[k] = jnp.broadcast_to(line, (128, 128)).T
    lib_charge = lcharge_ref[...].astype(F32)[part : part + 1, :]
    products = lax.dot_general(
        rows_ref[...], unit_ref[...], (((1,), (1,)), ((), ())), preferred_element_type=F32
    )
    for k in range(4):
        row_charge = charge_ref[k, pl.ds(at, seen), :][:, 0:1]
        kept = jnp.abs(row_charge - lib_charge) <= 2.0
        scores = jnp.where(kept, products[k * seen : (k + 1) * seen, :], 0.0).astype(BF16)
        if part:
            out_refs[k][:seen, :] = upper_refs[k][...]
        out_refs[k][part * seen : (part + 1) * seen, :] = scores


def home_kernel(me_ref, slot_ref, *refs):
    near8, near12, near4, near0, far8, far4, far12, far0, out_ref, flat_ref = refs
    near = [near0, near4, near8, near12]
    far = [far0, far4, far8, far12]
    q_rows = slot_ref.shape[1]
    l_rows = near0.shape[1]
    n_slab = 4 * PLANE
    total = n_slab * CAP
    slot = slot_ref[...]
    bucket, rank = slot // CAP, slot % CAP
    places = lax.broadcasted_iota(jnp.int32, (total, q_rows), 0)
    for unit in range(3):
        for m in range(n_slab):
            ref = (far if m & 2 else near)[m // PLANE]
            at = (m & 1) * 3 * CAP + (2 - unit) * CAP
            flat_ref[m * CAP : (m + 1) * CAP, :] = ref[at : at + CAP, :]
        slab = (bucket + (unit - 1 + n_slab)) % n_slab
        want = (slab ^ me_ref[0]) * CAP + rank
        select = jnp.where(places == want, 1.0, 0.0).T.astype(BF16)
        out_ref[:, unit * l_rows : (unit + 1) * l_rows] = jnp.dot(
            select, flat_ref[...], preferred_element_type=F32
        ).astype(BF16)


VMEM = pl.BlockSpec(memory_space=pltpu.VMEM)
SMEM = pl.BlockSpec(memory_space=pltpu.SMEM)


MIB = 1024 * 1024


def kernel_call(body, outs, args, specs, scratch=(), cost=1):
    return pl.pallas_call(
        body,
        out_shape=[jax.ShapeDtypeStruct(o.shape, o.dtype) for o in outs],
        in_specs=specs,
        out_specs=[VMEM] * len(outs),
        scratch_shapes=scratch,
        compiler_params=pltpu.CompilerParams(vmem_limit_bytes=12 * MIB),
        cost_estimate=pl.CostEstimate(flops=0, bytes_accessed=cost, transcendentals=0),
    )(*args)


def shape(*dims, dtype=BF16):
    return jax.ShapeDtypeStruct(dims, dtype)


def line_plan(queries, library, bucket, query_charge, library_charge):
    q_rows, width = queries.shape
    l_rows = library.shape[0]
    me = lax.axis_index("slab").astype(jnp.int32).reshape(1)
    n_slots, seen = (PLANE + 2) * CAP, 3 * CAP
    int32 = jnp.int32
    raw_y, raw_c = swapped(library, 2), swapped(library, 1)
    slot, qcharge, charge = kernel_call(
        slot_kernel,
        [shape(1, q_rows, dtype=int32), shape(META, q_rows), shape(META, l_rows)],
        [x.reshape(1, -1) for x in (bucket, query_charge, library_charge)],
        [VMEM] * 3,
        cost=1,
    )
    slots_shape = shape(width // 128 * n_slots + META, 128)
    q0, q4, q8, q12 = kernel_call(
        query_kernel,
        [slots_shape] * 3 + [shape(width // 128 * (n_slots - 2 * CAP) + META, 128)],
        [me, slot, qcharge, queries],
        [SMEM] + [VMEM] * 3,
    )
    q12, q8, q4 = swapped(q12, 12), swapped(q8, 8), swapped(q4, 4)
    lib = shape(l_rows, width)
    unit, unit_c = kernel_call(unit_kernel, [lib] * 2, [library, raw_c], [VMEM] * 2)
    charge_c = swapped(charge, 1)
    (near_charge,) = kernel_call(pair_kernel, [charge], [charge, charge_c], [VMEM] * 2)
    far_charge = swapped(near_charge, 2)

    block = shape(2 * seen, l_rows)
    shared_rows = width // l_rows * 2 * CAP + META + 32
    first = [q8, q4, q0, near_charge, unit, unit_c]
    near8, near4, near0, passed = kernel_call(
        first_kernel,
        [block] * 3 + [shape(shared_rows, l_rows)],
        [me, *first],
        [SMEM] + [VMEM] * len(first),
        [pltpu.VMEM((3 * seen, width), BF16), pltpu.VMEM((3, 128, 128), F32)],
    )
    near8, passed = swapped(near8, 8), swapped(passed, 4)
    near12, q12 = kernel_call(
        second_kernel,
        [block, slots_shape],
        [me, q12, passed, near_charge, unit, unit_c],
        [SMEM] + [VMEM] * 5,
        [
            pltpu.VMEM((seen, width), BF16),
            pltpu.VMEM((1, 128, 128), F32),
            pltpu.VMEM((3, 128, 128), F32),
        ],
    )
    near4 = swapped(near4, 4)
    raw_y, near8, near4, near12, far_charge = lax.optimization_barrier(
        (raw_y, near8, near4, near12, far_charge)
    )
    raw_d = swapped(raw_y, 1)
    near12 = swapped(near12, 12)
    upper = ()
    for part, raw in enumerate((raw_y, raw_d)):
        upper = kernel_call(
            functools.partial(far_kernel, part),
            [shape((part + 1) * seen, l_rows)] * 4,
            [me, q8, q4, q12, q0, far_charge, raw, *upper],
            [SMEM] + [VMEM] * (6 + len(upper)),
            [
                pltpu.VMEM((4 * seen, width), BF16),
                pltpu.VMEM((4, 128, 128), F32),
                pltpu.VMEM((l_rows, width), BF16),
            ],
        )
    far8, far4, far12, far0 = upper
    far8, far4, far12 = swapped(far8, 8), swapped(far4, 4), swapped(far12, 12)
    (out,) = kernel_call(
        home_kernel,
        [shape(q_rows, 3 * l_rows)],
        [me, slot, near8, near12, near4, near0, far8, far4, far12, far0],
        [SMEM] + [VMEM] * 9,
        [pltpu.VMEM((4 * PLANE * CAP, l_rows), BF16)],
    )
    return out


def per_device(queries, library, bucket, query_charge, library_charge):
    n_slab = lax.axis_size("slab")
    q_rows, width = queries.shape
    fits = n_slab == 4 * PLANE and 2 * q_rows == n_slab * CAP and q_rows == 128
    plan = line_plan if fits and width % 256 == 0 and width % (2 * library.shape[0]) == 0 else general_plan
    return plan(queries, library, bucket, query_charge, library_charge)


def solution(mesh):
    placed = (
        P(("grp", "slab"), None),
        P(("grp", "slab"), None),
        P(("grp", "slab"), None),
        P(("grp", "slab")),
        P(("grp", "slab")),
    )
    return jax.shard_map(
        per_device, mesh=mesh, in_specs=placed, out_specs=P(("grp", "slab"), None), check_vma=False
    )
```

```python
import functools

import jax
import jax.numpy as jnp
from jax import lax
from jax.experimental import pallas as pl
from jax.experimental.pallas import tpu as pltpu
from jax.sharding import PartitionSpec as P

EPS = 1e-06
PLANE = 4
CAP = 16
META = 16
F32 = jnp.float32
BF16 = jnp.bfloat16


def passed_along(value, axis, steps):
    count = lax.axis_size(axis)
    pairs = [(source, (source + steps) % count) for source in range(count)]
    return lax.ppermute(value, axis, pairs)


def normalize(rows):
    values = rows.astype(F32)
    return (values * lax.rsqrt(jnp.sum(values * values, axis=-1, keepdims=True) + EPS)).astype(BF16)


def score_block(rows, row_charge, lib_rows, lib_charge):
    raw = lax.dot_general(rows, lib_rows, (((1,), (1,)), ((), ())), preferred_element_type=F32)
    keep = jnp.abs(row_charge.astype(F32)[:, None] - lib_charge.astype(F32)[None, :]) <= 2.0
    return jnp.where(keep, raw, 0.0).astype(BF16)


def selector(slot_ids, total):
    places = jnp.arange(total, dtype=jnp.int32)
    return (places[:, None] == slot_ids[None, :]).astype(BF16)


def pick_rows(select, flat):
    return lax.dot_general(
        select, flat, (((0,), (0,)), ((), ())), preferred_element_type=F32
    ).astype(BF16)


def place_rows(select, values):
    return jnp.dot(select, values, preferred_element_type=F32).astype(BF16)


def general_plan(queries, library, bucket, query_charge, library_charge):
    n_slab = lax.axis_size("slab")
    q_rows = queries.shape[0]
    width = queries.shape[1]
    cap = 2 * q_rows // n_slab
    query_unit = normalize(queries)
    library_unit = normalize(library)
    lib_charge = library_charge.astype(BF16)
    qcharge_col = query_charge.astype(BF16)[:, None]
    target = bucket[:, 0]
    positions = jnp.arange(q_rows, dtype=jnp.int32)
    earlier = (target[:, None] == target[None, :]) & (positions[None, :] < positions[:, None])
    rank = jnp.sum(earlier.astype(jnp.int32), axis=1)
    select_home = selector(target * cap + rank, n_slab * cap)
    outgoing = place_rows(select_home, query_unit).reshape(n_slab, cap, width)
    out_charge = place_rows(select_home, qcharge_col).reshape(n_slab, cap)
    below_rows, below_charge = passed_along((library_unit, lib_charge), "slab", 1)
    above_rows, above_charge = passed_along((library_unit, lib_charge), "slab", -1)
    rows = lax.all_to_all(outgoing, "slab", split_axis=0, concat_axis=0, tiled=True)
    charges = lax.all_to_all(out_charge, "slab", split_axis=0, concat_axis=0, tiled=True)
    count = rows.shape[1]
    flat = rows.reshape(n_slab * count, width)
    flat_charge = charges.reshape(n_slab * count)
    middle = score_block(flat, flat_charge, library_unit, lib_charge)
    lower = score_block(flat, flat_charge, below_rows, below_charge)
    upper = score_block(flat, flat_charge, above_rows, above_charge)
    joined = jnp.concatenate([lower, middle, upper], axis=1)
    joined = joined.reshape(n_slab, count, joined.shape[1])
    returned = lax.all_to_all(joined, "slab", split_axis=0, concat_axis=0, tiled=True)
    flat_back = returned.reshape(returned.shape[0] * returned.shape[1], returned.shape[2])
    return pick_rows(select_home, flat_back)


def swapped(value, mask):
    count = lax.axis_size("slab")
    return lax.ppermute(value, "slab", [(i, i ^ mask) for i in range(count)])


def unit_rows(values):
    values = values.astype(F32)
    return (values * lax.rsqrt(jnp.sum(values * values, axis=-1, keepdims=True) + EPS)).astype(BF16)


def slot_kernel(bucket_ref, qcharge_ref, lcharge_ref, slot_ref, qcharge_out, lcharge_out):
    q_rows = bucket_ref.shape[1]
    bucket = bucket_ref[...]
    along = jnp.broadcast_to(bucket.astype(F32), (q_rows, q_rows))
    i = lax.broadcasted_iota(jnp.int32, (q_rows, q_rows), 0)
    j = lax.broadcasted_iota(jnp.int32, (q_rows, q_rows), 1)
    earlier = jnp.where((along == along.T) & (i < j), 1.0, 0.0)
    rank = jnp.sum(earlier, axis=0, keepdims=True)
    slot_ref[...] = bucket * CAP + rank.astype(jnp.int32)
    for source, target in ((qcharge_ref, qcharge_out), (lcharge_ref, lcharge_out)):
        target[...] = jnp.broadcast_to(source[...].astype(F32), target.shape).astype(BF16)


def query_kernel(me_ref, slot_ref, charge_ref, q_ref, *out_refs):
    q_rows, width = q_ref.shape
    n_slots = (PLANE + 2) * CAP
    total = 4 * PLANE * CAP
    unit = unit_rows(q_ref[...])
    for k in range(4):
        plane = (me_ref[0] // PLANE) ^ k
        count = n_slots if k < 3 else n_slots - 2 * CAP
        skip = plane % 2 * (2 * CAP) if k == 3 else 0
        rel = (slot_ref[...] + (total - (plane * PLANE - 1) * CAP)) % total - skip
        place = lax.broadcasted_iota(jnp.int32, (q_rows, q_rows), 0) == rel
        select = jnp.where(place, 1.0, 0.0).astype(BF16)
        rows = jnp.dot(select[:count, :], unit, preferred_element_type=F32).astype(BF16)
        for n in range(width // 128):
            out_refs[k][n * count : (n + 1) * count, :] = rows[:, n * 128 : (n + 1) * 128]
        placed = lax.dot_general(
            charge_ref[...], select, (((1,), (1,)), ((), ())), preferred_element_type=F32
        )
        out_refs[k][width // 128 * count :, :] = placed.astype(BF16)


def unit_kernel(*refs):
    count = len(refs) // 2
    for source, target in zip(refs[:count], refs[count:]):
        for start in range(0, source.shape[0], 64):
            target[start : start + 64, :] = unit_rows(source[start : start + 64, :])


def pair_kernel(one_ref, other_ref, out_ref):
    line = lax.broadcasted_iota(jnp.int32, out_ref.shape, 0)
    one, other = one_ref[...].astype(F32), other_ref[...].astype(F32)
    out_ref[...] = jnp.where(line == 0, one, other).astype(BF16)


def score_kernel(count, turn, me_ref, *refs):
    q_refs, refs = refs[:count], refs[count:]
    lcharge_ref, lib_refs, out_refs = refs[0], refs[1:3], refs[3 : 3 + count]
    rows_ref, charge_ref = refs[3 + count :]
    n_slots, seen = (PLANE + 2) * CAP, 3 * CAP
    for n, lib in enumerate(lib_refs):
        width = lib.shape[1]
        at = pl.multiple_of(((me_ref[0] % PLANE) ^ (turn ^ n)) * CAP, CAP)
        for k in range(count):
            for c in range(width // 128):
                rows_ref[k * seen : (k + 1) * seen, c * 128 : (c + 1) * 128] = q_refs[k][
                    pl.ds(pl.multiple_of(at + c * n_slots, CAP), seen), :
                ]
            if n == 0:
                line = q_refs[k][width // 128 * n_slots :, :].astype(F32)[0:1, :]
                charge_ref[k] = jnp.broadcast_to(line, (128, 128)).T
        lib_charge = lcharge_ref[...].astype(F32)[n : n + 1, :]
        products = lax.dot_general(
            rows_ref[...], lib[...], (((1,), (1,)), ((), ())), preferred_element_type=F32
        )
        for k in range(count):
            row_charge = charge_ref[k, pl.ds(at, seen), :][:, 0:1]
            kept = jnp.abs(row_charge - lib_charge) <= 2.0
            out_refs[k][n * seen : (n + 1) * seen, :] = jnp.where(
                kept, products[k * seen : (k + 1) * seen, :], 0.0
            ).astype(BF16)


def first_kernel(me_ref, *refs):
    score_kernel(3, 0, me_ref, *refs[:9], *refs[10:])
    q_ref, out_ref = refs[0], refs[9]
    n_slots, shared = (PLANE + 2) * CAP, 2 * CAP
    count = (q_ref.shape[0] - META) // n_slots
    at = (1 - me_ref[0] // PLANE % 2) * (n_slots - shared)
    wide = out_ref.shape[1] // 128
    for n in range(count):
        row, column = n // wide * shared, n % wide * 128
        out_ref[row : row + shared, column : column + 128] = q_ref[
            pl.ds(pl.multiple_of(at + n * n_slots, CAP), shared), :
        ]
    row = count // wide * shared
    out_ref[row:, :] = jnp.zeros((out_ref.shape[0] - row, out_ref.shape[1]), BF16)
    out_ref[row : row + META, :128] = q_ref[count * n_slots :, :]


def second_kernel(me_ref, q_ref, passed_ref, *refs):
    charge_refs, lib_refs, out_ref, block_ref = refs[0], refs[1:3], refs[3], refs[4]
    rows_ref, charge_ref, column_ref = refs[5:]
    n_slots, shared = (PLANE + 2) * CAP, 2 * CAP
    part = n_slots - shared
    count = (q_ref.shape[0] - META) // part
    wide = passed_ref.shape[1] // 128
    odd = me_ref[0] // PLANE % 2
    own_at, passed_at = odd * shared, (1 - odd) * part
    for n in range(count):
        row, column = n // wide * shared, n % wide * 128
        block_ref[pl.ds(pl.multiple_of(n * n_slots + own_at, CAP), part), :] = q_ref[
            n * part : (n + 1) * part, :
        ]
        block_ref[pl.ds(pl.multiple_of(n * n_slots + passed_at, CAP), shared), :] = passed_ref[
            row : row + shared, column : column + 128
        ]
    row = count // wide * shared
    own_line = q_ref[count * part :, :].astype(F32)[0:1, :]
    passed_line = passed_ref[row:, :128].astype(F32)[0:1, :]
    column_ref[0] = jnp.broadcast_to(passed_line, (128, 128)).T
    column_ref[1] = jnp.broadcast_to(own_line, (128, 128)).T
    column_ref[2] = jnp.zeros((128, 128), F32)
    column_ref[2, pl.ds(pl.multiple_of(own_at, CAP), part), :] = column_ref[1, :part, :]
    column_ref[2, pl.ds(pl.multiple_of(passed_at, CAP), shared), :] = column_ref[
        0, pl.ds(pl.multiple_of(odd * part, CAP), shared), :
    ]
    block_ref[count * n_slots :, :] = column_ref[2].T[:META, :].astype(BF16)
    score_kernel(1, 0, me_ref, block_ref, charge_refs, *lib_refs, out_ref, rows_ref, charge_ref)


def far_kernel(part, me_ref, *refs):
    q_refs, lcharge_ref, raw_ref, refs = refs[:4], refs[4], refs[5], refs[6:]
    upper_refs, refs = (refs[:4], refs[4:]) if part else ((), refs)
    out_refs, (rows_ref, charge_ref, unit_ref) = refs[:4], refs[4:]
    n_slots, seen = (PLANE + 2) * CAP, 3 * CAP
    for start in range(0, raw_ref.shape[0], 64):
        unit_ref[start : start + 64, :] = unit_rows(raw_ref[start : start + 64, :])
    at = pl.multiple_of(((me_ref[0] % PLANE) ^ (2 + part)) * CAP, CAP)
    chunks = raw_ref.shape[1] // 128
    for k in range(4):
        for c in range(chunks):
            rows_ref[k * seen : (k + 1) * seen, c * 128 : (c + 1) * 128] = q_refs[k][
                pl.ds(pl.multiple_of(at + c * n_slots, CAP), seen), :
            ]
        line = q_refs[k][chunks * n_slots :, :].astype(F32)[0:1, :]
        charge_ref[k] = jnp.broadcast_to(line, (128, 128)).T
    lib_charge = lcharge_ref[...].astype(F32)[part : part + 1, :]
    products = lax.dot_general(
        rows_ref[...], unit_ref[...], (((1,), (1,)), ((), ())), preferred_element_type=F32
    )
    for k in range(4):
        row_charge = charge_ref[k, pl.ds(at, seen), :][:, 0:1]
        kept = jnp.abs(row_charge - lib_charge) <= 2.0
        scores = jnp.where(kept, products[k * seen : (k + 1) * seen, :], 0.0).astype(BF16)
        if part:
            out_refs[k][:seen, :] = upper_refs[k][...]
        out_refs[k][part * seen : (part + 1) * seen, :] = scores


def select_kernel(me_ref, slot_ref, out_ref):
    q_rows, n_slab, total = slot_ref.shape[1], 4 * PLANE, 4 * PLANE * CAP
    slot = slot_ref[...]
    bucket, rank = slot // CAP, slot % CAP
    places = lax.broadcasted_iota(jnp.int32, (total, q_rows), 0)
    for unit in range(3):
        slab = (bucket + (unit - 1 + n_slab)) % n_slab
        want = (slab ^ me_ref[0]) * CAP + rank
        out_ref[unit] = jnp.where(places == want, 1.0, 0.0).T.astype(BF16)


def home_kernel(select_ref, *refs):
    near8, near12, near4, near0, far8, far4, far12, far0, out_hbm, flat_ref, out_ref, sem = refs
    near = [near0, near4, near8, near12]
    far = [far0, far4, far8, far12]
    l_rows = near0.shape[1]
    copies = []
    for unit in range(3):
        for m in range(4 * PLANE):
            ref = (far if m & 2 else near)[m // PLANE]
            at = (m & 1) * 3 * CAP + (2 - unit) * CAP
            flat_ref[unit, m * CAP : (m + 1) * CAP, :] = ref[at : at + CAP, :]
        out_ref[unit] = jnp.dot(
            select_ref[unit], flat_ref[unit], preferred_element_type=F32
        ).astype(BF16)
        columns = pl.ds(unit * l_rows, l_rows)
        copies.append(pltpu.make_async_copy(out_ref.at[unit], out_hbm.at[:, columns], sem.at[unit]))
        copies[unit].start()
    for copy in copies:
        copy.wait()


VMEM = pl.BlockSpec(memory_space=pltpu.VMEM)
SMEM = pl.BlockSpec(memory_space=pltpu.SMEM)


MIB = 1024 * 1024


def kernel_call(body, outs, args, specs, scratch=(), out_spec=VMEM):
    return pl.pallas_call(
        body,
        out_shape=[jax.ShapeDtypeStruct(o.shape, o.dtype) for o in outs],
        in_specs=specs,
        out_specs=[out_spec] * len(outs),
        scratch_shapes=scratch,
        compiler_params=pltpu.CompilerParams(vmem_limit_bytes=12 * MIB),
        cost_estimate=pl.CostEstimate(flops=0, bytes_accessed=1, transcendentals=0),
    )(*args)


def shape(*dims, dtype=BF16):
    return jax.ShapeDtypeStruct(dims, dtype)


def line_plan(queries, library, bucket, query_charge, library_charge):
    q_rows, width = queries.shape
    l_rows = library.shape[0]
    me = lax.axis_index("slab").astype(jnp.int32).reshape(1)
    n_slots, seen = (PLANE + 2) * CAP, 3 * CAP
    int32 = jnp.int32
    raw_y, raw_c = swapped(library, 2), swapped(library, 1)
    slot, qcharge, charge = kernel_call(
        slot_kernel,
        [shape(1, q_rows, dtype=int32), shape(META, q_rows), shape(META, l_rows)],
        [x.reshape(1, -1) for x in (bucket, query_charge, library_charge)],
        [VMEM] * 3,
    )
    slots_shape = shape(width // 128 * n_slots + META, 128)
    q0, q4, q8, q12 = kernel_call(
        query_kernel,
        [slots_shape] * 3 + [shape(width // 128 * (n_slots - 2 * CAP) + META, 128)],
        [me, slot, qcharge, queries],
        [SMEM] + [VMEM] * 3,
    )
    q12, q8, q4 = swapped(q12, 12), swapped(q8, 8), swapped(q4, 4)
    lib = shape(l_rows, width)
    unit, unit_c = kernel_call(unit_kernel, [lib] * 2, [library, raw_c], [VMEM] * 2)
    charge_c = swapped(charge, 1)
    (near_charge,) = kernel_call(pair_kernel, [charge], [charge, charge_c], [VMEM] * 2)
    far_charge = swapped(near_charge, 2)

    block = shape(2 * seen, l_rows)
    shared_rows = width // l_rows * 2 * CAP + META + 32
    first = [q8, q4, q0, near_charge, unit, unit_c]
    near8, near4, near0, passed = kernel_call(
        first_kernel,
        [block] * 3 + [shape(shared_rows, l_rows)],
        [me, *first],
        [SMEM] + [VMEM] * len(first),
        [pltpu.VMEM((3 * seen, width), BF16), pltpu.VMEM((3, 128, 128), F32)],
    )
    near8, passed = swapped(near8, 8), swapped(passed, 4)
    near12, q12 = kernel_call(
        second_kernel,
        [block, slots_shape],
        [me, q12, passed, near_charge, unit, unit_c],
        [SMEM] + [VMEM] * 5,
        [
            pltpu.VMEM((seen, width), BF16),
            pltpu.VMEM((1, 128, 128), F32),
            pltpu.VMEM((3, 128, 128), F32),
        ],
    )
    near4 = swapped(near4, 4)
    (select,) = kernel_call(
        select_kernel, [shape(3, q_rows, 4 * PLANE * CAP)], [me, slot], [SMEM, VMEM]
    )
    raw_y, near8, near4, near12, far_charge, select = lax.optimization_barrier(
        (raw_y, near8, near4, near12, far_charge, select)
    )
    raw_d = swapped(raw_y, 1)
    near12 = swapped(near12, 12)
    upper = ()
    for part, raw in enumerate((raw_y, raw_d)):
        upper = kernel_call(
            functools.partial(far_kernel, part),
            [shape((part + 1) * seen, l_rows)] * 4,
            [me, q8, q4, q12, q0, far_charge, raw, *upper],
            [SMEM] + [VMEM] * (6 + len(upper)),
            [
                pltpu.VMEM((4 * seen, width), BF16),
                pltpu.VMEM((4, 128, 128), F32),
                pltpu.VMEM((l_rows, width), BF16),
            ],
        )
    far8, far4, far12, far0 = upper
    far8, far4, far12 = swapped(far8, 8), swapped(far4, 4), swapped(far12, 12)
    (out,) = kernel_call(
        home_kernel,
        [shape(q_rows, 3 * l_rows)],
        [select, near8, near12, near4, near0, far8, far4, far12, far0],
        [VMEM] * 9,
        [
            pltpu.VMEM((3, 4 * PLANE * CAP, l_rows), BF16),
            pltpu.VMEM((3, q_rows, l_rows), BF16),
            pltpu.SemaphoreType.DMA((3,)),
        ],
        out_spec=pl.BlockSpec(memory_space=pl.ANY),
    )
    return out


def per_device(queries, library, bucket, query_charge, library_charge):
    n_slab = lax.axis_size("slab")
    q_rows, width = queries.shape
    fits = n_slab == 4 * PLANE and 2 * q_rows == n_slab * CAP and q_rows == 128
    plan = line_plan if fits and width % 256 == 0 and width % (2 * library.shape[0]) == 0 else general_plan
    return plan(queries, library, bucket, query_charge, library_charge)


def solution(mesh):
    placed = (
        P(("grp", "slab"), None),
        P(("grp", "slab"), None),
        P(("grp", "slab"), None),
        P(("grp", "slab")),
        P(("grp", "slab")),
    )
    return jax.shard_map(
        per_device, mesh=mesh, in_specs=placed, out_specs=P(("grp", "slab"), None), check_vma=False
    )
```

```python
import functools

import jax
import jax.numpy as jnp
from jax import lax
from jax.experimental import pallas as pl
from jax.experimental.pallas import tpu as pltpu
from jax.sharding import PartitionSpec as P

EPS = 1e-06
PLANE = 4
CAP = 16
META = 16
F32 = jnp.float32
BF16 = jnp.bfloat16


def passed_along(value, axis, steps):
    count = lax.axis_size(axis)
    pairs = [(source, (source + steps) % count) for source in range(count)]
    return lax.ppermute(value, axis, pairs)


def normalize(rows):
    values = rows.astype(F32)
    return (values * lax.rsqrt(jnp.sum(values * values, axis=-1, keepdims=True) + EPS)).astype(BF16)


def score_block(rows, row_charge, lib_rows, lib_charge):
    raw = lax.dot_general(rows, lib_rows, (((1,), (1,)), ((), ())), preferred_element_type=F32)
    keep = jnp.abs(row_charge.astype(F32)[:, None] - lib_charge.astype(F32)[None, :]) <= 2.0
    return jnp.where(keep, raw, 0.0).astype(BF16)


def selector(slot_ids, total):
    places = jnp.arange(total, dtype=jnp.int32)
    return (places[:, None] == slot_ids[None, :]).astype(BF16)


def pick_rows(select, flat):
    return lax.dot_general(
        select, flat, (((0,), (0,)), ((), ())), preferred_element_type=F32
    ).astype(BF16)


def place_rows(select, values):
    return jnp.dot(select, values, preferred_element_type=F32).astype(BF16)


def general_plan(queries, library, bucket, query_charge, library_charge):
    n_slab = lax.axis_size("slab")
    q_rows = queries.shape[0]
    width = queries.shape[1]
    cap = 2 * q_rows // n_slab
    query_unit = normalize(queries)
    library_unit = normalize(library)
    lib_charge = library_charge.astype(BF16)
    qcharge_col = query_charge.astype(BF16)[:, None]
    target = bucket[:, 0]
    positions = jnp.arange(q_rows, dtype=jnp.int32)
    earlier = (target[:, None] == target[None, :]) & (positions[None, :] < positions[:, None])
    rank = jnp.sum(earlier.astype(jnp.int32), axis=1)
    select_home = selector(target * cap + rank, n_slab * cap)
    outgoing = place_rows(select_home, query_unit).reshape(n_slab, cap, width)
    out_charge = place_rows(select_home, qcharge_col).reshape(n_slab, cap)
    below_rows, below_charge = passed_along((library_unit, lib_charge), "slab", 1)
    above_rows, above_charge = passed_along((library_unit, lib_charge), "slab", -1)
    rows = lax.all_to_all(outgoing, "slab", split_axis=0, concat_axis=0, tiled=True)
    charges = lax.all_to_all(out_charge, "slab", split_axis=0, concat_axis=0, tiled=True)
    count = rows.shape[1]
    flat = rows.reshape(n_slab * count, width)
    flat_charge = charges.reshape(n_slab * count)
    middle = score_block(flat, flat_charge, library_unit, lib_charge)
    lower = score_block(flat, flat_charge, below_rows, below_charge)
    upper = score_block(flat, flat_charge, above_rows, above_charge)
    joined = jnp.concatenate([lower, middle, upper], axis=1)
    joined = joined.reshape(n_slab, count, joined.shape[1])
    returned = lax.all_to_all(joined, "slab", split_axis=0, concat_axis=0, tiled=True)
    flat_back = returned.reshape(returned.shape[0] * returned.shape[1], returned.shape[2])
    return pick_rows(select_home, flat_back)


def swapped(value, mask):
    count = lax.axis_size("slab")
    return lax.ppermute(value, "slab", [(i, i ^ mask) for i in range(count)])


def unit_rows(values):
    values = values.astype(F32)
    return (values * lax.rsqrt(jnp.sum(values * values, axis=-1, keepdims=True) + EPS)).astype(BF16)


def slot_kernel(bucket_ref, qcharge_ref, lcharge_ref, slot_ref, qcharge_out, lcharge_out):
    q_rows = bucket_ref.shape[1]
    bucket = bucket_ref[...]
    along = jnp.broadcast_to(bucket.astype(F32), (q_rows, q_rows))
    i = lax.broadcasted_iota(jnp.int32, (q_rows, q_rows), 0)
    j = lax.broadcasted_iota(jnp.int32, (q_rows, q_rows), 1)
    earlier = jnp.where((along == along.T) & (i < j), 1.0, 0.0)
    rank = jnp.sum(earlier, axis=0, keepdims=True)
    slot_ref[...] = bucket * CAP + rank.astype(jnp.int32)
    for source, target in ((qcharge_ref, qcharge_out), (lcharge_ref, lcharge_out)):
        target[...] = jnp.broadcast_to(source[...].astype(F32), target.shape).astype(BF16)


def query_kernel(me_ref, slot_ref, charge_ref, q_ref, *out_refs):
    q_rows, width = q_ref.shape
    n_slots = (PLANE + 2) * CAP
    total = 4 * PLANE * CAP
    unit = unit_rows(q_ref[...])
    for k in range(4):
        plane = (me_ref[0] // PLANE) ^ k
        count = n_slots if k < 3 else n_slots - 2 * CAP
        skip = plane % 2 * (2 * CAP) if k == 3 else 0
        rel = (slot_ref[...] + (total - (plane * PLANE - 1) * CAP)) % total - skip
        place = lax.broadcasted_iota(jnp.int32, (q_rows, q_rows), 0) == rel
        select = jnp.where(place, 1.0, 0.0).astype(BF16)
        rows = jnp.dot(select[:count, :], unit, preferred_element_type=F32).astype(BF16)
        for n in range(width // 128):
            out_refs[k][n * count : (n + 1) * count, :] = rows[:, n * 128 : (n + 1) * 128]
        placed = lax.dot_general(
            charge_ref[...], select, (((1,), (1,)), ((), ())), preferred_element_type=F32
        )
        out_refs[k][width // 128 * count :, :] = placed.astype(BF16)


def unit_kernel(*refs):
    count = len(refs) // 2
    for source, target in zip(refs[:count], refs[count:]):
        for start in range(0, source.shape[0], 64):
            target[start : start + 64, :] = unit_rows(source[start : start + 64, :])


def pair_kernel(one_ref, other_ref, out_ref):
    line = lax.broadcasted_iota(jnp.int32, out_ref.shape, 0)
    one, other = one_ref[...].astype(F32), other_ref[...].astype(F32)
    out_ref[...] = jnp.where(line == 0, one, other).astype(BF16)


def score_kernel(count, turn, me_ref, *refs):
    q_refs, refs = refs[:count], refs[count:]
    lcharge_ref, lib_refs, out_refs = refs[0], refs[1:3], refs[3 : 3 + count]
    rows_ref, charge_ref = refs[3 + count :]
    n_slots, seen = (PLANE + 2) * CAP, 3 * CAP
    for n, lib in enumerate(lib_refs):
        width = lib.shape[1]
        at = pl.multiple_of(((me_ref[0] % PLANE) ^ (turn ^ n)) * CAP, CAP)
        for k in range(count):
            for c in range(width // 128):
                rows_ref[k * seen : (k + 1) * seen, c * 128 : (c + 1) * 128] = q_refs[k][
                    pl.ds(pl.multiple_of(at + c * n_slots, CAP), seen), :
                ]
            if n == 0:
                line = q_refs[k][width // 128 * n_slots :, :].astype(F32)[0:1, :]
                charge_ref[k] = jnp.broadcast_to(line, (128, 128)).T
        lib_charge = lcharge_ref[...].astype(F32)[n : n + 1, :]
        products = lax.dot_general(
            rows_ref[...], lib[...], (((1,), (1,)), ((), ())), preferred_element_type=F32
        )
        for k in range(count):
            row_charge = charge_ref[k, pl.ds(at, seen), :][:, 0:1]
            kept = jnp.abs(row_charge - lib_charge) <= 2.0
            out_refs[k][n * seen : (n + 1) * seen, :] = jnp.where(
                kept, products[k * seen : (k + 1) * seen, :], 0.0
            ).astype(BF16)


def first_kernel(me_ref, *refs):
    score_kernel(2, 0, me_ref, *refs[:7], *refs[8:])
    q_ref, out_ref = refs[0], refs[7]
    n_slots, shared = (PLANE + 2) * CAP, 2 * CAP
    count = (q_ref.shape[0] - META) // n_slots
    at = (1 - me_ref[0] // PLANE % 2) * (n_slots - shared)
    wide = out_ref.shape[1] // 128
    for n in range(count):
        row, column = n // wide * shared, n % wide * 128
        out_ref[row : row + shared, column : column + 128] = q_ref[
            pl.ds(pl.multiple_of(at + n * n_slots, CAP), shared), :
        ]
    row = count // wide * shared
    out_ref[row:, :] = jnp.zeros((out_ref.shape[0] - row, out_ref.shape[1]), BF16)
    out_ref[row : row + META, :128] = q_ref[count * n_slots :, :]


def second_kernel(me_ref, q_ref, passed_ref, own_ref, *refs):
    charge_refs, lib_refs, out_refs, block_ref = refs[0], refs[1:3], refs[3:5], refs[5]
    rows_ref, charge_ref, column_ref = refs[6:]
    n_slots, shared = (PLANE + 2) * CAP, 2 * CAP
    part = n_slots - shared
    count = (q_ref.shape[0] - META) // part
    wide = passed_ref.shape[1] // 128
    odd = me_ref[0] // PLANE % 2
    own_at, passed_at = odd * shared, (1 - odd) * part
    for n in range(count):
        row, column = n // wide * shared, n % wide * 128
        block_ref[pl.ds(pl.multiple_of(n * n_slots + own_at, CAP), part), :] = q_ref[
            n * part : (n + 1) * part, :
        ]
        block_ref[pl.ds(pl.multiple_of(n * n_slots + passed_at, CAP), shared), :] = passed_ref[
            row : row + shared, column : column + 128
        ]
    row = count // wide * shared
    own_line = q_ref[count * part :, :].astype(F32)[0:1, :]
    passed_line = passed_ref[row:, :128].astype(F32)[0:1, :]
    column_ref[0] = jnp.broadcast_to(passed_line, (128, 128)).T
    column_ref[1] = jnp.broadcast_to(own_line, (128, 128)).T
    column_ref[2] = jnp.zeros((128, 128), F32)
    column_ref[2, pl.ds(pl.multiple_of(own_at, CAP), part), :] = column_ref[1, :part, :]
    column_ref[2, pl.ds(pl.multiple_of(passed_at, CAP), shared), :] = column_ref[
        0, pl.ds(pl.multiple_of(odd * part, CAP), shared), :
    ]
    block_ref[count * n_slots :, :] = column_ref[2].T[:META, :].astype(BF16)
    q_refs = (block_ref, own_ref)
    score_kernel(2, 0, me_ref, *q_refs, charge_refs, *lib_refs, *out_refs, rows_ref, charge_ref)


def far_kernel(part, me_ref, *refs):
    q_refs, lcharge_ref, raw_ref, refs = refs[:4], refs[4], refs[5], refs[6:]
    upper_refs, refs = (refs[:4], refs[4:]) if part else ((), refs)
    out_refs, (rows_ref, charge_ref, unit_ref) = refs[:4], refs[4:]
    n_slots, seen = (PLANE + 2) * CAP, 3 * CAP
    for start in range(0, raw_ref.shape[0], 64):
        unit_ref[start : start + 64, :] = unit_rows(raw_ref[start : start + 64, :])
    at = pl.multiple_of(((me_ref[0] % PLANE) ^ (2 + part)) * CAP, CAP)
    chunks = raw_ref.shape[1] // 128
    for k in range(4):
        for c in range(chunks):
            rows_ref[k * seen : (k + 1) * seen, c * 128 : (c + 1) * 128] = q_refs[k][
                pl.ds(pl.multiple_of(at + c * n_slots, CAP), seen), :
            ]
        line = q_refs[k][chunks * n_slots :, :].astype(F32)[0:1, :]
        charge_ref[k] = jnp.broadcast_to(line, (128, 128)).T
    lib_charge = lcharge_ref[...].astype(F32)[part : part + 1, :]
    products = lax.dot_general(
        rows_ref[...], unit_ref[...], (((1,), (1,)), ((), ())), preferred_element_type=F32
    )
    for k in range(4):
        row_charge = charge_ref[k, pl.ds(at, seen), :][:, 0:1]
        kept = jnp.abs(row_charge - lib_charge) <= 2.0
        scores = jnp.where(kept, products[k * seen : (k + 1) * seen, :], 0.0).astype(BF16)
        if part:
            out_refs[k][:seen, :] = upper_refs[k][...]
        out_refs[k][part * seen : (part + 1) * seen, :] = scores


def select_kernel(me_ref, slot_ref, out_ref):
    q_rows, n_slab, total = slot_ref.shape[1], 4 * PLANE, 4 * PLANE * CAP
    slot = slot_ref[...]
    bucket, rank = slot // CAP, slot % CAP
    places = lax.broadcasted_iota(jnp.int32, (total, q_rows), 0)
    for unit in range(3):
        slab = (bucket + (unit - 1 + n_slab)) % n_slab
        want = (slab ^ me_ref[0]) * CAP + rank
        out_ref[unit] = jnp.where(places == want, 1.0, 0.0).T.astype(BF16)


def home_kernel(select_ref, *refs):
    near8, near12, near4, near0, far8, far4, far12, far0, out_hbm, flat_ref, out_ref, sem = refs
    near = [near0, near4, near8, near12]
    far = [far0, far4, far8, far12]
    l_rows = near0.shape[1]
    copies = []
    for unit in range(3):
        for m in range(4 * PLANE):
            ref = (far if m & 2 else near)[m // PLANE]
            at = (m & 1) * 3 * CAP + (2 - unit) * CAP
            flat_ref[unit, m * CAP : (m + 1) * CAP, :] = ref[at : at + CAP, :]
        out_ref[unit] = jnp.dot(
            select_ref[unit], flat_ref[unit], preferred_element_type=F32
        ).astype(BF16)
        columns = pl.ds(unit * l_rows, l_rows)
        copies.append(pltpu.make_async_copy(out_ref.at[unit], out_hbm.at[:, columns], sem.at[unit]))
        copies[unit].start()
    for copy in copies:
        copy.wait()


VMEM = pl.BlockSpec(memory_space=pltpu.VMEM)
SMEM = pl.BlockSpec(memory_space=pltpu.SMEM)


MIB = 1024 * 1024


def kernel_call(body, outs, args, specs, scratch=(), out_spec=VMEM):
    return pl.pallas_call(
        body,
        out_shape=[jax.ShapeDtypeStruct(o.shape, o.dtype) for o in outs],
        in_specs=specs,
        out_specs=[out_spec] * len(outs),
        scratch_shapes=scratch,
        compiler_params=pltpu.CompilerParams(vmem_limit_bytes=12 * MIB),
        cost_estimate=pl.CostEstimate(flops=0, bytes_accessed=1, transcendentals=0),
    )(*args)


def shape(*dims, dtype=BF16):
    return jax.ShapeDtypeStruct(dims, dtype)


def line_plan(queries, library, bucket, query_charge, library_charge):
    q_rows, width = queries.shape
    l_rows = library.shape[0]
    me = lax.axis_index("slab").astype(jnp.int32).reshape(1)
    n_slots, seen = (PLANE + 2) * CAP, 3 * CAP
    int32 = jnp.int32
    raw_y, raw_c = swapped(library, 2), swapped(library, 1)
    slot, qcharge, charge = kernel_call(
        slot_kernel,
        [shape(1, q_rows, dtype=int32), shape(META, q_rows), shape(META, l_rows)],
        [x.reshape(1, -1) for x in (bucket, query_charge, library_charge)],
        [VMEM] * 3,
    )
    slots_shape = shape(width // 128 * n_slots + META, 128)
    q0, q4, q8, q12 = kernel_call(
        query_kernel,
        [slots_shape] * 3 + [shape(width // 128 * (n_slots - 2 * CAP) + META, 128)],
        [me, slot, qcharge, queries],
        [SMEM] + [VMEM] * 3,
    )
    q12, q8, q4 = swapped(q12, 12), swapped(q8, 8), swapped(q4, 4)
    lib = shape(l_rows, width)
    unit, unit_c = kernel_call(unit_kernel, [lib] * 2, [library, raw_c], [VMEM] * 2)
    charge_c = swapped(charge, 1)
    (near_charge,) = kernel_call(pair_kernel, [charge], [charge, charge_c], [VMEM] * 2)
    far_charge = swapped(near_charge, 2)

    block = shape(2 * seen, l_rows)
    shared_rows = width // l_rows * 2 * CAP + META + 32
    first = [q8, q4, near_charge, unit, unit_c]
    near8, near4, passed = kernel_call(
        first_kernel,
        [block] * 2 + [shape(shared_rows, l_rows)],
        [me, *first],
        [SMEM] + [VMEM] * len(first),
        [pltpu.VMEM((2 * seen, width), BF16), pltpu.VMEM((2, 128, 128), F32)],
    )
    near8, passed = swapped(near8, 8), swapped(passed, 4)
    near12, near0, q12 = kernel_call(
        second_kernel,
        [block, block, slots_shape],
        [me, q12, passed, q0, near_charge, unit, unit_c],
        [SMEM] + [VMEM] * 6,
        [
            pltpu.VMEM((2 * seen, width), BF16),
            pltpu.VMEM((2, 128, 128), F32),
            pltpu.VMEM((3, 128, 128), F32),
        ],
    )
    near4 = swapped(near4, 4)
    (select,) = kernel_call(
        select_kernel, [shape(3, q_rows, 4 * PLANE * CAP)], [me, slot], [SMEM, VMEM]
    )
    raw_y, near8, near4, near12, far_charge, select = lax.optimization_barrier(
        (raw_y, near8, near4, near12, far_charge, select)
    )
    raw_d = swapped(raw_y, 1)
    near12 = swapped(near12, 12)
    upper = ()
    for part, raw in enumerate((raw_y, raw_d)):
        upper = kernel_call(
            functools.partial(far_kernel, part),
            [shape((part + 1) * seen, l_rows)] * 4,
            [me, q8, q4, q12, q0, far_charge, raw, *upper],
            [SMEM] + [VMEM] * (6 + len(upper)),
            [
                pltpu.VMEM((4 * seen, width), BF16),
                pltpu.VMEM((4, 128, 128), F32),
                pltpu.VMEM((l_rows, width), BF16),
            ],
        )
    far8, far4, far12, far0 = upper
    far8, far4, far12 = swapped(far8, 8), swapped(far4, 4), swapped(far12, 12)
    (out,) = kernel_call(
        home_kernel,
        [shape(q_rows, 3 * l_rows)],
        [select, near8, near12, near4, near0, far8, far4, far12, far0],
        [VMEM] * 9,
        [
            pltpu.VMEM((3, 4 * PLANE * CAP, l_rows), BF16),
            pltpu.VMEM((3, q_rows, l_rows), BF16),
            pltpu.SemaphoreType.DMA((3,)),
        ],
        out_spec=pl.BlockSpec(memory_space=pl.ANY),
    )
    return out


def per_device(queries, library, bucket, query_charge, library_charge):
    n_slab = lax.axis_size("slab")
    q_rows, width = queries.shape
    fits = n_slab == 4 * PLANE and 2 * q_rows == n_slab * CAP and q_rows == 128
    plan = line_plan if fits and width % 256 == 0 and width % (2 * library.shape[0]) == 0 else general_plan
    return plan(queries, library, bucket, query_charge, library_charge)


def solution(mesh):
    placed = (
        P(("grp", "slab"), None),
        P(("grp", "slab"), None),
        P(("grp", "slab"), None),
        P(("grp", "slab")),
        P(("grp", "slab")),
    )
    return jax.shard_map(
        per_device, mesh=mesh, in_specs=placed, out_specs=P(("grp", "slab"), None), check_vma=False
    )
```
